128 devices in a mesh: tok: 8 (over y_hi, x), voc: 16 (over z, y_lo, core).
Axes of the slice: x: 4, y: 4 (y_hi: 2, y_lo: 2; y = y_hi * 2 + y_lo), z: 4, core: 2. Of those that a mesh axis runs over, the one named last changes fastest.
Arguments:
- hidden: bfloat16 [6144, 4096], P('tok', 'voc')
- weight: bfloat16 [81920, 4096], P('voc', 'tok')
- targets: int32 [6144], P('tok'), may hold values from 0 to 81919, as said below
- cotangent: float32 [6144], P('tok'), may hold values from 1 to 10
- kept_blocks: int32 [8, 16, 2], P(None, 'voc'), may hold values from 0 to 9, as said below
- kept_counts: int32 [8, 16], P(None, 'voc'), may hold values from 0 to 2, as said below
Outputs:
- d_hidden: bfloat16 [6144, 4096], P('tok', 'voc')
- d_weight: bfloat16 [81920, 4096], P('voc', 'tok')
The draws below stay inside these ranges and needn't reach their ends.
Inputs may be any that keep to these rules, and one draw needn't show every extreme that they name: `kept_blocks`: entries are local block numbers of the shard; the first kept_counts entries of a list are distinct, the rest are 0. `kept_counts`: in every token block some shards reach 2; the same shards do so in every token block. `targets`: every target lies in a kept block of its token block.
All inputs are finite; a program needn't handle non-finite values.
Results may differ from the reference program's by a relative error of at most 0.0055.
Values may be sent and summed in bfloat16 or wider, within the bound.
No kernel may reach another device: no remote copies, remote signals or barrier semaphores. Data moves between devices by JAX's collectives and lax.ppermute only.
A program may use at most 128 MiB of HBM per device.

```python
import math
import jax
import jax.numpy as jnp
from jax import lax

D = 4096
BLOCK = 512
VBLK_DEV = 10
KMAX = 2
TOK_DEV = 768
TOKENS = 6144
V = 81920
N_TOK = 8
N_VOC = 16


def kept_core(key):
    base = jax.random.fold_in(key, 11)
    first, second, third = jax.random.split(base, 3)
    order = jax.random.permutation(first, N_VOC)
    frequent = order < max(1, N_VOC // 5)
    others = jnp.minimum(jax.random.randint(second, (N_TOK, N_VOC), 0, KMAX + 1), KMAX - 1)
    counts = jnp.where(frequent[None, :], KMAX, others).astype(jnp.int32)
    scores = jax.random.randint(third, (N_TOK, N_VOC, VBLK_DEV), 0, 1 << 20) * VBLK_DEV + jnp.arange(VBLK_DEV, dtype=jnp.int32)
    picks = jnp.argsort(scores, axis=-1)[..., :KMAX].astype(jnp.int32)
    kept = jnp.where(jnp.arange(KMAX, dtype=jnp.int32)[None, None, :] < counts[..., None], picks, 0)
    return (kept.astype(jnp.int32), counts)


def target_core(key):
    kept, counts = kept_core(key)
    first, second = jax.random.split(jax.random.fold_in(key, 12))
    entries = N_VOC * KMAX
    live = (jnp.arange(KMAX, dtype=jnp.int32)[None, None, :] < counts[..., None]).reshape(N_TOK, entries).astype(jnp.int32)
    number = jnp.sum(live, axis=1)
    pick = jax.random.randint(first, (N_TOK, TOK_DEV), 0, 1 << 20) % number[:, None]
    rank = jnp.cumsum(live, axis=1) - 1
    match = (live[:, None, :] == 1) & (rank[:, None, :] == pick[:, :, None])
    index = jnp.sum(jnp.where(match, jnp.arange(entries, dtype=jnp.int32)[None, None, :], 0), axis=-1)
    shard = index // KMAX
    local = jnp.take_along_axis(kept.reshape(N_TOK, entries), index, axis=1)
    offset = jax.random.randint(second, (N_TOK, TOK_DEV), 0, BLOCK)
    return ((shard * VBLK_DEV + local) * BLOCK + offset).reshape(TOKENS).astype(jnp.int32)


def weight_core(key):
    first = jax.random.fold_in(jax.random.fold_in(key, 21), 0)
    drawn = jax.random.normal(first, (V, D), jnp.float32) * (3.0 / D ** 0.5)
    return drawn


def draw_kept_blocks(key, part):
    return kept_core(key)[0]


def draw_kept_counts(key, part):
    return kept_core(key)[1]


def draw_targets(key, part):
    return target_core(key)


def draw_weight(key, part):
    mixed = weight_core(key)
    return mixed.astype(jnp.bfloat16)


def draw_hidden(key, part):
    first = jax.random.fold_in(jax.random.fold_in(key, 31), 0)
    values = jax.random.normal(first, (TOKENS, D), jnp.float32)
    return values.astype(jnp.bfloat16)


def levels(rng, dims, cuts, smallest, top_value):
    gain, own = 1.0, jax.random.fold_in(rng, 6)
    for position, blocks in cuts:
        heights = jnp.exp(jax.random.uniform(jax.random.fold_in(own, position), (blocks,), jnp.float32, smallest / len(cuts), top_value / len(cuts)))
        gain = gain * jnp.repeat(heights, dims[position] // blocks).reshape([-1 if axis == position else 1 for axis in range(len(dims))])
    return gain


def setup_inputs(seed: int = 0) -> dict:
    arg_keys = jax.random.split(jax.random.key(seed), 7)
    hidden = draw_hidden(jax.random.fold_in(arg_keys[6], 71), 0)
    weight = draw_weight(jax.random.fold_in(arg_keys[6], 71), 0)
    targets = draw_targets(jax.random.fold_in(arg_keys[6], 71), 0)
    cotangent = jnp.clip(jnp.exp(math.log(10.0) - 2.3025851 * jax.random.uniform(arg_keys[3], (TOKENS,), jnp.float32) ** levels(arg_keys[3], (TOKENS,), ((0, 8),), -0.2, 0.2)), 1.0, 10.0)
    kept_blocks = draw_kept_blocks(jax.random.fold_in(arg_keys[6], 71), 0)
    kept_counts = draw_kept_counts(jax.random.fold_in(arg_keys[6], 71), 0)
    return dict(hidden=hidden, weight=weight, targets=targets, cotangent=cotangent, kept_blocks=kept_blocks, kept_counts=kept_counts)


def reference(hidden, weight, targets, cotangent, kept_blocks, kept_counts):
    blocks_h = hidden.reshape(N_TOK, TOK_DEV, D)
    blocks_t = targets.reshape(N_TOK, TOK_DEV)
    blocks_c = cotangent.reshape(N_TOK, TOK_DEV)
    offsets = jnp.arange(BLOCK, dtype=jnp.int32)

    def one_block(total, inputs):
        feats, tgt, cot, lists, counts = inputs
        global_blocks = jnp.arange(N_VOC, dtype=jnp.int32)[:, None] * VBLK_DEV + lists.astype(jnp.int32)
        row_ids = (global_blocks[:, :, None] * BLOCK + offsets[None, None, :]).reshape(-1).astype(jnp.int32)
        live = jnp.broadcast_to((jnp.arange(KMAX, dtype=jnp.int32)[None, :] < counts[:, None])[:, :, None], (N_VOC, KMAX, BLOCK)).reshape(-1)
        rows = weight[row_ids]
        logits = jnp.dot(feats, rows.T, preferred_element_type=jnp.float32)
        masked = jnp.where(live[None, :], logits, jnp.float32(-1e30))
        top = jnp.max(masked, axis=1)
        summed = jnp.sum(jnp.where(live[None, :], jnp.exp(masked - top[:, None]), jnp.float32(0.0)), axis=1)
        lse = top + jnp.log(summed)
        prob = jnp.where(live[None, :], jnp.exp(logits - lse[:, None]), jnp.float32(0.0))
        hit = jnp.where((row_ids[None, :] == tgt[:, None]) & live[None, :], jnp.float32(1.0), jnp.float32(0.0))
        grad = (cot[:, None] * (prob - hit)).astype(jnp.bfloat16)
        d_feats = jnp.dot(grad, rows, preferred_element_type=jnp.float32).astype(jnp.bfloat16)
        part = jnp.dot(grad.T, feats, preferred_element_type=jnp.float32).astype(jnp.bfloat16)
        total = total.at[row_ids].add(part.astype(jnp.float32))
        return total, d_feats

    start = jnp.zeros((V, D), jnp.float32)
    total, d_blocks = lax.scan(one_block, start, (blocks_h, blocks_t, blocks_c, kept_blocks, kept_counts))
    return d_blocks.reshape(TOKENS, D), total.astype(jnp.bfloat16)
```

```python
import functools

import jax
import jax.numpy as jnp
from jax import lax
from jax.experimental import pallas as pl
from jax.experimental.pallas import tpu as pltpu
from jax.sharding import PartitionSpec as P

BLOCK = 512
KMAX = 2
NEG = -1e30
F32 = jnp.float32
BF16 = jnp.bfloat16
VMEM_LIMIT = 56 * 1024 * 1024
NZ, NY, NC = 4, 2, 2
NT = (((1,), (1,)), ((), ()))
NN = (((1,), (0,)), ((), ()))


def call(kernel, name, prefetch, grid, in_specs, out_specs, out_shape, scratch=(), flops=0, moved=0):
    return pl.pallas_call(
        kernel,
        grid_spec=pltpu.PrefetchScalarGridSpec(
            num_scalar_prefetch=prefetch,
            grid=grid,
            in_specs=in_specs,
            out_specs=out_specs,
            scratch_shapes=list(scratch),
        ),
        out_shape=out_shape,
        compiler_params=pltpu.CompilerParams(vmem_limit_bytes=VMEM_LIMIT),
        cost_estimate=pl.CostEstimate(flops=flops, bytes_accessed=moved, transcendentals=0),
        name=name,
    )


def dot(a, b, dims):
    return lax.dot_general(a, b, dims, preferred_element_type=F32)


class Meta:
    def __init__(self, tok_count, nblk):
        self.tok_count, self.nblk = tok_count, nblk

    def block(self, m, t, slot):
        return m[t * KMAX + slot]

    def kept(self, m, t):
        return m[self.tok_count * KMAX + t]

    def tok(self, m):
        return m[self.tok_count * (KMAX + 1)]

    def voc(self, m):
        return m[self.tok_count * (KMAX + 1) + 1]

    def core(self, m):
        return lax.rem(self.voc(m), NC)

    def y(self, m):
        return lax.rem(lax.div(self.voc(m), NC), NY)

    def count(self, m):
        return self.kept(m, self.tok(m))

    def start(self, m, slot):
        return (self.voc(m) * self.nblk + self.block(m, self.tok(m), slot)) * BLOCK

    def z(self, m):
        return lax.div(self.voc(m), NC * NY)

    def held(self, m, k, e):
        return lax.rem(self.z(m) + NZ - k, NZ) * NY + jnp.bitwise_xor(self.y(m), e)

    def owed(self, m, k, e):
        return lax.rem(self.z(m) + k, NZ) * NY + e


def gather_kernel(m, first, second, out):
    out[0, :BLOCK, :] = first[0]
    out[0, BLOCK:, :] = second[0]


def gather_call(meta, lists, weight):
    _, rows, columns = weight.shape
    shape = (meta.tok_count, KMAX * rows, columns)
    return call(
        gather_kernel,
        "gather",
        1,
        (meta.tok_count,),
        [
            pl.BlockSpec((1, rows, columns), lambda t, m, s=slot: (meta.block(m, t, s), 0, 0))
            for slot in range(KMAX)
        ],
        pl.BlockSpec((1, KMAX * rows, columns), lambda t, m: (t, 0, 0)),
        jax.ShapeDtypeStruct(shape, BF16),
        moved=4 * meta.tok_count * KMAX * rows * columns,
    )(lists, weight, weight)


def pair_kernel(hidden, near, tiles, out):
    del tiles
    out[0] = hidden[...]
    out[1] = near[...]


def pair_call(hidden, near, tiles):
    whole = pl.BlockSpec(hidden.shape, lambda: (0, 0))
    return call(
        pair_kernel,
        "pair",
        0,
        (),
        [whole, whole, pl.BlockSpec(memory_space=pl.ANY)],
        pl.BlockSpec((NY, *hidden.shape), lambda: (0, 0, 0)),
        jax.ShapeDtypeStruct((NY, *hidden.shape), hidden.dtype),
        moved=8 * hidden.size,
    )(hidden, near, tiles)


def hold(arrays, behind):
    n = len(arrays)
    anywhere = pl.BlockSpec(memory_space=pl.ANY)
    return pl.pallas_call(
        lambda *refs: None,
        in_specs=[anywhere] * (n + 1),
        out_specs=[anywhere] * n,
        out_shape=[jax.ShapeDtypeStruct(a.shape, a.dtype) for a in arrays],
        input_output_aliases={i: i for i in range(n)},
        compiler_params=pltpu.CompilerParams(vmem_limit_bytes=VMEM_LIMIT),
        name="hold",
    )(*arrays, behind)


def tile_logits(meta, m, pieces, w):
    values = None
    for k, piece in enumerate(pieces):
        for e in range(NY):
            part = dot(w[meta.held(m, k, e)], piece[e], NT)
            values = part if values is None else values + part
    return values


def near_kernel(meta, tile, m, p0, p1, p2, p3, w, logits):
    @pl.when(pl.program_id(0) * tile < meta.count(m) * BLOCK)
    def _():
        logits[...] = tile_logits(meta, m, (p0, p1, p2, p3), w)


def far_kernel(meta, tile, m, p0, p1, p2, p3, w, near, logits, stats):
    @pl.when(pl.program_id(0) == 0)
    def _():
        stats[0:1, :] = jnp.full(stats[0:1, :].shape, NEG, F32)
        stats[1:2, :] = jnp.zeros(stats[1:2, :].shape, F32)

    @pl.when(pl.program_id(0) * tile < meta.count(m) * BLOCK)
    def _():
        values = near[...] + tile_logits(meta, m, (p0, p1, p2, p3), w)
        logits[...] = values
        old = stats[0:1, :]
        top = jnp.maximum(old, jnp.max(values, axis=0, keepdims=True))
        own = jnp.sum(jnp.exp(values - top), axis=0, keepdims=True)
        stats[1:2, :] = stats[1:2, :] * jnp.exp(old - top) + own
        stats[0:1, :] = top


def logits_call(meta, m, pieces, w, near=None):
    chunks, width, columns = w.shape
    _, tokens, half = pieces[0].shape
    tile = 256
    block = pl.BlockSpec((tile, tokens), lambda i, m: (i, 0))
    shape = jax.ShapeDtypeStruct((width, tokens), F32)
    far = near is not None
    return call(
        functools.partial(far_kernel if far else near_kernel, meta, tile),
        "logits_far" if far else "logits_near",
        1,
        (width // tile,),
        [pl.BlockSpec(p.shape, lambda i, m: (0, 0, 0)) for p in pieces]
        + [
            pl.BlockSpec(
                (chunks, tile, half),
                lambda i, m: (0, i, 1 - meta.core(m) if far else meta.core(m)),
            )
        ]
        + [block] * far,
        [block, pl.BlockSpec((2, tokens), lambda i, m: (0, 0))] if far else block,
        [shape, jax.ShapeDtypeStruct((2, tokens), F32)] if far else shape,
        flops=width * tokens * chunks * columns,
        moved=width * chunks * columns + 4 * width * tokens,
    )(m, *pieces, w, *[near] * far)


def other_kernel(meta, m, logits, s0, s1, s2, s3, cot, targets, w, grad_t, grad, other):
    count = meta.count(m)

    @pl.when(pl.program_id(0) == 0)
    def _():
        parts = [s0[...], s1[...], s2[...], s3[...]]
        top = functools.reduce(jnp.maximum, [s[0:1, :] for s in parts])
        lse = top + jnp.log(sum(s[1:2, :] * jnp.exp(s[0:1, :] - top) for s in parts))
        for slot in range(KMAX):
            rows = pl.ds(slot * BLOCK, BLOCK)

            @pl.when(slot < count)
            def _(slot=slot, rows=rows):
                prob = jnp.exp(logits[rows, :] - lse)
                place = lax.broadcasted_iota(jnp.int32, prob.shape, 0)
                hit = place == targets[...] - meta.start(m, slot)
                value = (cot[...] * (prob - jnp.where(hit, 1.0, 0.0))).astype(BF16)
                grad_t[rows, :] = value
                grad[:, rows] = value.T

    @pl.when(count == 0)
    def _():
        other[...] = jnp.zeros(other.shape, BF16)

    @pl.when(count == 1)
    def _():
        other[0] = dot(grad[:, :BLOCK], w[0, :BLOCK, :], NN).astype(BF16)

    @pl.when(count > 1)
    def _():
        other[0] = dot(grad[...], w[0], NN).astype(BF16)


def other_call(meta, m, logits, stats, cot, targets, w):
    chunks, width, columns = w.shape
    half = columns // NC
    tokens = logits.shape[1]
    whole = lambda c, m: (0, 0)
    row = pl.BlockSpec((1, tokens), whole)
    return call(
        functools.partial(other_kernel, meta),
        "hidden_other",
        1,
        (chunks,),
        [
            pl.BlockSpec((width, tokens), whole),
            *[pl.BlockSpec((2, tokens), whole)] * 4,
            row,
            row,
            pl.BlockSpec((1, width, half), lambda c, m: (c, 0, 1 - meta.core(m))),
        ],
        [
            pl.BlockSpec((width, tokens), whole),
            pl.BlockSpec((tokens, width), whole),
            pl.BlockSpec((1, tokens, half), lambda c, m: (c, 0, 0)),
        ],
        [
            jax.ShapeDtypeStruct((width, tokens), BF16),
            jax.ShapeDtypeStruct((tokens, width), BF16),
            jax.ShapeDtypeStruct((chunks, tokens, half), BF16),
        ],
        flops=width * tokens * chunks * columns,
        moved=w.size + 4 * logits.size,
    )(m, logits, *stats, cot, targets, w)


def rows_kernel(meta, m, grad_t, *refs):
    out = refs[-1]
    pieces, others = refs[:NZ], refs[NZ : 2 * NZ]
    step = pl.program_id(0)
    halves = (pl.ds(0, pieces[0].shape[-1]), pl.ds(pieces[0].shape[-1], pieces[0].shape[-1]))
    for k in range(NZ):
        for core in range(NC):

            @pl.when((step // NY == k) & (meta.core(m) == core) & (meta.count(m) > 0))
            def _(k=k, core=core):
                out[0, :, halves[core]] = dot(grad_t[...], pieces[k][0], NN).astype(BF16)
                out[0, :, halves[1 - core]] = dot(grad_t[...], others[k][0], NN).astype(BF16)


def rows_call(meta, m, grad_t, pieces, others):
    width, tokens = grad_t.shape
    half = pieces[0].shape[-1]
    chunks = NZ * NY
    specs = [
        pl.BlockSpec((1, tokens, half), lambda i, m, k=k: (jnp.clip(i - NY * k, 0, NY - 1), 0, 0))
        for k in range(NZ)
    ]
    return call(
        functools.partial(rows_kernel, meta),
        "head_rows",
        1,
        (chunks,),
        [pl.BlockSpec((width, tokens), lambda i, m: (0, 0))] + specs + specs,
        pl.BlockSpec(
            (1, width, NC * half), lambda i, m: (meta.held(m, i // NY, lax.rem(i, NY)), 0, 0)
        ),
        jax.ShapeDtypeStruct((chunks, width, NC * half), BF16),
        flops=2 * width * tokens * chunks * NC * half,
        moved=2 * chunks * width * NC * half,
    )(m, grad_t, *pieces, *others)


def mine_kernel(meta, m, grad, w, got, rows, *outs):
    del rows
    count = meta.count(m)
    step = pl.program_id(0)

    def put(value):
        for k, out in enumerate(outs):

            @pl.when(step // NY == k)
            def _(out=out):
                out[0] = value.astype(out.dtype)

    @pl.when(count == 0)
    def _():
        put(got[0].astype(F32))

    @pl.when(count == 1)
    def _():
        put(got[0].astype(F32) + dot(grad[:, :BLOCK], w[0, :BLOCK, :], NN))

    @pl.when(count > 1)
    def _():
        put(got[0].astype(F32) + dot(grad[...], w[0], NN))


def mine_call(meta, m, grad, w, got, rows):
    chunks, width, columns = w.shape
    half = columns // NC
    tokens = grad.shape[0]

    def chunk(i, m):
        return meta.owed(m, i // NY, lax.rem(i, NY))

    return call(
        functools.partial(mine_kernel, meta),
        "hidden_mine",
        1,
        (chunks,),
        [
            pl.BlockSpec((tokens, width), lambda i, m: (0, 0)),
            pl.BlockSpec((1, width, half), lambda i, m: (chunk(i, m), 0, meta.core(m))),
            pl.BlockSpec((1, tokens, half), lambda i, m: (chunk(i, m), 0, 0)),
            pl.BlockSpec(memory_space=pl.ANY),
        ],
        [
            pl.BlockSpec((1, tokens, half), lambda i, m, k=k: (jnp.clip(i - NY * k, 0, NY - 1), 0, 0))
            for k in range(NZ)
        ],
        [jax.ShapeDtypeStruct((NY, tokens, half), BF16 if k else F32) for k in range(NZ)],
        flops=width * tokens * chunks * columns,
        moved=w.size,
    )(m, grad, w, got, rows)


def combine_kernel(meta, m, pieces, out, total):
    for block in range(meta.nblk):
        total[...] = jnp.zeros(total.shape, F32)
        for t in range(meta.tok_count):
            for slot in range(KMAX):

                @pl.when((meta.block(m, t, slot) == block) & (slot < meta.kept(m, t)))
                def _(t=t, slot=slot):
                    total[...] += pieces[t, slot * BLOCK : (slot + 1) * BLOCK, :].astype(F32)

        out[block] = total[...].astype(BF16)


def combine_call(meta, m, pieces):
    tok_count, width, columns = pieces.shape
    part = 128
    return call(
        functools.partial(combine_kernel, meta),
        "combine",
        1,
        (columns // part,),
        [pl.BlockSpec((tok_count, width, part), lambda c, m: (0, 0, c))],
        pl.BlockSpec((meta.nblk, BLOCK, part), lambda c, m: (0, 0, c)),
        jax.ShapeDtypeStruct((meta.nblk, BLOCK, columns), BF16),
        [pltpu.VMEM((BLOCK, part), F32)],
        moved=2 * pieces.size + 2 * meta.nblk * BLOCK * columns,
    )(m, pieces)


def pick_kernel(meta, m, *refs):
    *parts, _, keep, away = refs
    y = meta.y(m)
    keep[...] = functools.reduce(jnp.add, [p[y].astype(F32) for p in parts])
    away[...] = functools.reduce(jnp.add, [p[1 - y].astype(F32) for p in parts]).astype(BF16)


def pick_call(meta, m, parts, returned):
    _, tokens, half = parts[0].shape
    whole = pl.BlockSpec((tokens, half), lambda i, m: (0, 0))
    return call(
        functools.partial(pick_kernel, meta),
        "pick",
        1,
        (1,),
        [pl.BlockSpec(p.shape, lambda i, m: (0, 0, 0)) for p in parts]
        + [pl.BlockSpec(memory_space=pl.ANY)],
        [whole, whole],
        [
            jax.ShapeDtypeStruct((tokens, half), F32),
            jax.ShapeDtypeStruct((tokens, half), BF16),
        ],
        moved=12 * NY * tokens * half,
    )(m, *parts, returned)


def merge(parts):
    top = functools.reduce(jnp.maximum, [s[0] for s in parts])
    return jnp.stack([top, sum(s[1] * jnp.exp(s[0] - top) for s in parts)])


def exchange(parts, frequent):
    def swap(x):
        return lax.all_to_all(x, "tok", split_axis=0, concat_axis=0, tiled=True)

    def small(x):
        rest = jnp.zeros((x.shape[0], x.shape[1] - BLOCK, x.shape[2]), x.dtype)
        return jnp.concatenate([swap(x[:, :BLOCK]), rest], axis=1)

    return lax.cond(frequent, swap, small, parts)


def local(hidden, weight, targets, cotangent, kept_blocks, kept_counts):
    tok_count = lax.axis_size("tok")
    voc_count = lax.axis_size("voc")
    tok_me = lax.axis_index("tok")
    voc_me = lax.axis_index("voc")
    stride = NC * NY

    def flip(x, bits):
        return lax.ppermute(x, "voc", [(i, i ^ bits) for i in range(voc_count)])

    def up(x, k):
        pairs = [(i, (i + k * stride) % voc_count) for i in range(voc_count)]
        return lax.ppermute(x, "voc", pairs) if k else x

    vrows, columns = weight.shape
    nblk = vrows // BLOCK
    lists = kept_blocks[:, 0, :].reshape(-1)
    counts = kept_counts[:, 0]
    frequent = jnp.any(counts > 1)
    meta = Meta(tok_count, nblk)
    m = jnp.concatenate([lists, counts, jnp.stack([tok_me, voc_me])]).astype(jnp.int32)

    tiles = gather_call(meta, m, weight.reshape(nblk, BLOCK, columns))
    pair = pair_call(hidden, flip(hidden, NC), tiles)
    pieces = [up(pair, k) for k in range(NZ)]
    w = exchange(tiles, frequent)
    pieces = [pair, *hold(pieces[1:], w)]
    others = [flip(piece, 1) for piece in pieces]

    near = logits_call(meta, m, pieces, w)
    logits, stats = logits_call(meta, m, others, w, near)
    stats = merge([up(stats, k) for k in range(NZ)])
    stats = [stats] + [flip(stats, bits) for bits in (1, NC, NC + 1)]
    grad_t, grad, other = other_call(
        meta, m, logits, stats, cotangent[None, :], targets[None, :], w
    )
    got = flip(other, 1)
    rows = rows_call(meta, m, grad_t, pieces, others)
    owed = mine_call(meta, m, grad, w, got, rows)
    parts = [up(part, k) for k, part in enumerate(owed)]
    returned = exchange(rows, frequent)
    keep, away = pick_call(meta, m, parts, returned)
    d_weight = combine_call(meta, m, returned)
    d_hidden = (keep + flip(away, NC).astype(F32)).astype(BF16)
    return (d_hidden, d_weight.reshape(vrows, columns))


def solution(mesh):
    placed = (
        P("tok", "voc"),
        P("voc", "tok"),
        P("tok"),
        P("tok"),
        P(None, "voc", None),
        P(None, "voc"),
    )
    return jax.shard_map(
        local,
        mesh=mesh,
        in_specs=placed,
        out_specs=(P("tok", "voc"), P("voc", "tok")),
        check_vma=False,
    )
```

```python
import functools

import jax
import jax.numpy as jnp
from jax import lax
from jax.experimental import pallas as pl
from jax.experimental.pallas import tpu as pltpu
from jax.sharding import PartitionSpec as P

BLOCK = 512
KMAX = 2
NEG = -1e30
F32 = jnp.float32
BF16 = jnp.bfloat16
VMEM_LIMIT = 22 * 1024 * 1024
NZ, NY, NC = 4, 2, 2
NT = (((1,), (1,)), ((), ()))
NN = (((1,), (0,)), ((), ()))


def call(kernel, name, prefetch, grid, in_specs, out_specs, out_shape, scratch=(), flops=0, moved=0):
    return pl.pallas_call(
        kernel,
        grid_spec=pltpu.PrefetchScalarGridSpec(
            num_scalar_prefetch=prefetch,
            grid=grid,
            in_specs=in_specs,
            out_specs=out_specs,
            scratch_shapes=list(scratch),
        ),
        out_shape=out_shape,
        compiler_params=pltpu.CompilerParams(vmem_limit_bytes=VMEM_LIMIT),
        cost_estimate=pl.CostEstimate(flops=flops, bytes_accessed=moved, transcendentals=0),
        name=name,
    )


def dot(a, b, dims):
    return lax.dot_general(a, b, dims, preferred_element_type=F32)


class Meta:
    def __init__(self, tok_count, nblk):
        self.tok_count, self.nblk = tok_count, nblk

    def block(self, m, t, slot):
        return m[t * KMAX + slot]

    def kept(self, m, t):
        return m[self.tok_count * KMAX + t]

    def tok(self, m):
        return m[self.tok_count * (KMAX + 1)]

    def voc(self, m):
        return m[self.tok_count * (KMAX + 1) + 1]

    def core(self, m):
        return lax.rem(self.voc(m), NC)

    def y(self, m):
        return lax.rem(lax.div(self.voc(m), NC), NY)

    def count(self, m):
        return self.kept(m, self.tok(m))

    def start(self, m, slot):
        return (self.voc(m) * self.nblk + self.block(m, self.tok(m), slot)) * BLOCK

    def z(self, m):
        return lax.div(self.voc(m), NC * NY)

    def held(self, m, k, e):
        return lax.rem(self.z(m) + NZ - k, NZ) * NY + jnp.bitwise_xor(self.y(m), e)

    def owed(self, m, k, e):
        return lax.rem(self.z(m) + k, NZ) * NY + e


def gather_kernel(m, first, second, out):
    out[0, :BLOCK, :] = first[0]
    out[0, BLOCK:, :] = second[0]


def gather_call(meta, lists, weight):
    _, rows, columns = weight.shape
    shape = (meta.tok_count, KMAX * rows, columns)
    return call(
        gather_kernel,
        "gather",
        1,
        (meta.tok_count,),
        [
            pl.BlockSpec((1, rows, columns), lambda t, m, s=slot: (meta.block(m, t, s), 0, 0))
            for slot in range(KMAX)
        ],
        pl.BlockSpec((1, KMAX * rows, columns), lambda t, m: (t, 0, 0)),
        jax.ShapeDtypeStruct(shape, BF16),
        moved=4 * meta.tok_count * KMAX * rows * columns,
    )(lists, weight, weight)


def pair_kernel(hidden, near, tiles, out):
    del tiles
    out[0] = hidden[...]
    out[1] = near[...]


def pair_call(hidden, near, tiles):
    whole = pl.BlockSpec(hidden.shape, lambda: (0, 0))
    return call(
        pair_kernel,
        "pair",
        0,
        (),
        [whole, whole, pl.BlockSpec(memory_space=pl.ANY)],
        pl.BlockSpec((NY, *hidden.shape), lambda: (0, 0, 0)),
        jax.ShapeDtypeStruct((NY, *hidden.shape), hidden.dtype),
        moved=8 * hidden.size,
    )(hidden, near, tiles)


def hold(arrays, behind):
    n = len(arrays)
    anywhere = pl.BlockSpec(memory_space=pl.ANY)
    return pl.pallas_call(
        lambda *refs: None,
        in_specs=[anywhere] * (n + 1),
        out_specs=[anywhere] * n,
        out_shape=[jax.ShapeDtypeStruct(a.shape, a.dtype) for a in arrays],
        input_output_aliases={i: i for i in range(n)},
        compiler_params=pltpu.CompilerParams(vmem_limit_bytes=VMEM_LIMIT),
        name="hold",
    )(*arrays, behind)


def tile_logits(meta, m, pieces, w):
    values = None
    for k, piece in enumerate(pieces):
        for e in range(NY):
            part = dot(w[meta.held(m, k, e)], piece[e], NT)
            values = part if values is None else values + part
    return values


def near_kernel(meta, tile, m, p0, p1, p2, p3, w, logits):
    @pl.when(pl.program_id(0) * tile < meta.count(m) * BLOCK)
    def _():
        logits[...] = tile_logits(meta, m, (p0, p1, p2, p3), w)


def far_kernel(meta, tile, m, p0, p1, p2, p3, w, near, logits, stats):
    @pl.when(pl.program_id(0) == 0)
    def _():
        stats[0:1, :] = jnp.full(stats[0:1, :].shape, NEG, F32)
        stats[1:2, :] = jnp.zeros(stats[1:2, :].shape, F32)

    @pl.when(pl.program_id(0) * tile < meta.count(m) * BLOCK)
    def _():
        values = near[...] + tile_logits(meta, m, (p0, p1, p2, p3), w)
        logits[...] = values
        old = stats[0:1, :]
        top = jnp.maximum(old, jnp.max(values, axis=0, keepdims=True))
        own = jnp.sum(jnp.exp(values - top), axis=0, keepdims=True)
        stats[1:2, :] = stats[1:2, :] * jnp.exp(old - top) + own
        stats[0:1, :] = top


def logits_call(meta, m, pieces, w, near=None):
    chunks, width, columns = w.shape
    _, tokens, half = pieces[0].shape
    tile = 256
    block = pl.BlockSpec((tile, tokens), lambda i, m: (i, 0))
    shape = jax.ShapeDtypeStruct((width, tokens), F32)
    far = near is not None
    return call(
        functools.partial(far_kernel if far else near_kernel, meta, tile),
        "logits_far" if far else "logits_near",
        1,
        (width // tile,),
        [pl.BlockSpec(p.shape, lambda i, m: (0, 0, 0)) for p in pieces]
        + [
            pl.BlockSpec(
                (chunks, tile, half),
                lambda i, m: (0, i, 1 - meta.core(m) if far else meta.core(m)),
            )
        ]
        + [block] * far,
        [block, pl.BlockSpec((2, tokens), lambda i, m: (0, 0))] if far else block,
        [shape, jax.ShapeDtypeStruct((2, tokens), F32)] if far else shape,
        flops=width * tokens * chunks * columns,
        moved=width * chunks * columns + 4 * width * tokens,
    )(m, *pieces, w, *[near] * far)


def other_kernel(meta, m, logits, s0, s1, s2, s3, cot, targets, w, grad_t, grad, other):
    count = meta.count(m)

    @pl.when(pl.program_id(0) == 0)
    def _():
        parts = [s0[...], s1[...], s2[...], s3[...]]
        top = functools.reduce(jnp.maximum, [s[0:1, :] for s in parts])
        lse = top + jnp.log(sum(s[1:2, :] * jnp.exp(s[0:1, :] - top) for s in parts))
        for slot in range(KMAX):
            rows = pl.ds(slot * BLOCK, BLOCK)

            @pl.when(slot < count)
            def _(slot=slot, rows=rows):
                prob = jnp.exp(logits[rows, :] - lse)
                place = lax.broadcasted_iota(jnp.int32, prob.shape, 0)
                hit = place == targets[...] - meta.start(m, slot)
                value = (cot[...] * (prob - jnp.where(hit, 1.0, 0.0))).astype(BF16)
                grad_t[rows, :] = value
                grad[:, rows] = value.T

    @pl.when(count == 0)
    def _():
        other[...] = jnp.zeros(other.shape, BF16)

    @pl.when(count == 1)
    def _():
        other[0] = dot(grad[:, :BLOCK], w[0, :BLOCK, :], NN).astype(BF16)

    @pl.when(count > 1)
    def _():
        other[0] = dot(grad[...], w[0], NN).astype(BF16)


def other_call(meta, m, logits, stats, cot, targets, w):
    chunks, width, columns = w.shape
    half = columns // NC
    tokens = logits.shape[1]
    whole = lambda c, m: (0, 0)
    row = pl.BlockSpec((1, tokens), whole)
    return call(
        functools.partial(other_kernel, meta),
        "hidden_other",
        1,
        (chunks,),
        [
            pl.BlockSpec((width, tokens), whole),
            *[pl.BlockSpec((2, tokens), whole)] * 4,
            row,
            row,
            pl.BlockSpec((1, width, half), lambda c, m: (c, 0, 1 - meta.core(m))),
        ],
        [
            pl.BlockSpec((width, tokens), whole),
            pl.BlockSpec((tokens, width), whole),
            pl.BlockSpec((1, tokens, half), lambda c, m: (c, 0, 0)),
        ],
        [
            jax.ShapeDtypeStruct((width, tokens), BF16),
            jax.ShapeDtypeStruct((tokens, width), BF16),
            jax.ShapeDtypeStruct((chunks, tokens, half), BF16),
        ],
        flops=width * tokens * chunks * columns,
        moved=w.size + 4 * logits.size,
    )(m, logits, *stats, cot, targets, w)


def rows_kernel(meta, m, grad_t, *refs):
    out = refs[-1]
    pieces, others = refs[:NZ], refs[NZ : 2 * NZ]
    step = pl.program_id(0)
    halves = (pl.ds(0, pieces[0].shape[-1]), pl.ds(pieces[0].shape[-1], pieces[0].shape[-1]))
    for k in range(NZ):
        for core in range(NC):

            for slot in range(KMAX):
                some = pl.ds(slot * BLOCK, BLOCK)

                @pl.when((step // NY == k) & (meta.core(m) == core) & (meta.count(m) > slot))
                def _(k=k, core=core, some=some):
                    grads = grad_t[some, :]
                    out[0, some, halves[core]] = dot(grads, pieces[k][0], NN).astype(BF16)
                    out[0, some, halves[1 - core]] = dot(grads, others[k][0], NN).astype(BF16)


def rows_call(meta, m, grad_t, pieces, others):
    width, tokens = grad_t.shape
    half = pieces[0].shape[-1]
    chunks = NZ * NY
    specs = [
        pl.BlockSpec((1, tokens, half), lambda i, m, k=k: (jnp.clip(i - NY * k, 0, NY - 1), 0, 0))
        for k in range(NZ)
    ]
    return call(
        functools.partial(rows_kernel, meta),
        "head_rows",
        1,
        (chunks,),
        [pl.BlockSpec((width, tokens), lambda i, m: (0, 0))] + specs + specs,
        pl.BlockSpec(
            (1, width, NC * half), lambda i, m: (meta.held(m, i // NY, lax.rem(i, NY)), 0, 0)
        ),
        jax.ShapeDtypeStruct((chunks, width, NC * half), BF16),
        flops=2 * width * tokens * chunks * NC * half,
        moved=2 * chunks * width * NC * half,
    )(m, grad_t, *pieces, *others)


def mine_kernel(meta, m, grad, w, got, rows, *outs):
    del rows
    count = meta.count(m)
    step = pl.program_id(0)

    def put(value):
        for k, out in enumerate(outs):

            @pl.when(step // NY == k)
            def _(out=out):
                out[0] = value.astype(out.dtype)

    @pl.when(count == 0)
    def _():
        put(got[0].astype(F32))

    @pl.when(count == 1)
    def _():
        put(got[0].astype(F32) + dot(grad[:, :BLOCK], w[0, :BLOCK, :], NN))

    @pl.when(count > 1)
    def _():
        put(got[0].astype(F32) + dot(grad[...], w[0], NN))


def mine_call(meta, m, grad, w, got, rows):
    chunks, width, columns = w.shape
    half = columns // NC
    tokens = grad.shape[0]

    def chunk(i, m):
        return meta.owed(m, i // NY, lax.rem(i, NY))

    return call(
        functools.partial(mine_kernel, meta),
        "hidden_mine",
        1,
        (chunks,),
        [
            pl.BlockSpec((tokens, width), lambda i, m: (0, 0)),
            pl.BlockSpec((1, width, half), lambda i, m: (chunk(i, m), 0, meta.core(m))),
            pl.BlockSpec((1, tokens, half), lambda i, m: (chunk(i, m), 0, 0)),
            pl.BlockSpec(memory_space=pl.ANY),
        ],
        [
            pl.BlockSpec((1, tokens, half), lambda i, m, k=k: (jnp.clip(i - NY * k, 0, NY - 1), 0, 0))
            for k in range(NZ)
        ],
        [jax.ShapeDtypeStruct((NY, tokens, half), BF16 if k else F32) for k in range(NZ)],
        flops=width * tokens * chunks * columns,
        moved=w.size,
    )(m, grad, w, got, rows)


def combine_kernel(meta, m, pieces, out, total):
    for block in range(meta.nblk):
        total[...] = jnp.zeros(total.shape, F32)
        for t in range(meta.tok_count):
            for slot in range(KMAX):

                @pl.when((meta.block(m, t, slot) == block) & (slot < meta.kept(m, t)))
                def _(t=t, slot=slot):
                    total[...] += pieces[t, slot * BLOCK : (slot + 1) * BLOCK, :].astype(F32)

        out[block] = total[...].astype(BF16)


def combine_call(meta, m, pieces):
    tok_count, width, columns = pieces.shape
    part = 128
    return call(
        functools.partial(combine_kernel, meta),
        "combine",
        1,
        (columns // part,),
        [pl.BlockSpec((tok_count, width, part), lambda c, m: (0, 0, c))],
        pl.BlockSpec((meta.nblk, BLOCK, part), lambda c, m: (0, 0, c)),
        jax.ShapeDtypeStruct((meta.nblk, BLOCK, columns), BF16),
        [pltpu.VMEM((BLOCK, part), F32)],
        moved=2 * pieces.size + 2 * meta.nblk * BLOCK * columns,
    )(m, pieces)


def pick_kernel(meta, m, *refs):
    *parts, _, keep, away = refs
    y = meta.y(m)
    keep[...] = functools.reduce(jnp.add, [p[y].astype(F32) for p in parts])
    away[...] = functools.reduce(jnp.add, [p[1 - y].astype(F32) for p in parts]).astype(BF16)


def pick_call(meta, m, parts, returned):
    _, tokens, half = parts[0].shape
    whole = pl.BlockSpec((tokens, half), lambda i, m: (0, 0))
    return call(
        functools.partial(pick_kernel, meta),
        "pick",
        1,
        (1,),
        [pl.BlockSpec(p.shape, lambda i, m: (0, 0, 0)) for p in parts]
        + [pl.BlockSpec(memory_space=pl.ANY)],
        [whole, whole],
        [
            jax.ShapeDtypeStruct((tokens, half), F32),
            jax.ShapeDtypeStruct((tokens, half), BF16),
        ],
        moved=12 * NY * tokens * half,
    )(m, *parts, returned)


def merge(parts):
    top = functools.reduce(jnp.maximum, [s[0] for s in parts])
    return jnp.stack([top, sum(s[1] * jnp.exp(s[0] - top) for s in parts)])


def exchange(parts, frequent):
    def swap(x):
        return lax.all_to_all(x, "tok", split_axis=0, concat_axis=0, tiled=True)

    def small(x):
        rest = jnp.zeros((x.shape[0], x.shape[1] - BLOCK, x.shape[2]), x.dtype)
        return jnp.concatenate([swap(x[:, :BLOCK]), rest], axis=1)

    return lax.cond(frequent, swap, small, parts)


def local(hidden, weight, targets, cotangent, kept_blocks, kept_counts):
    tok_count = lax.axis_size("tok")
    voc_count = lax.axis_size("voc")
    tok_me = lax.axis_index("tok")
    voc_me = lax.axis_index("voc")
    stride = NC * NY

    def flip(x, bits):
        return lax.ppermute(x, "voc", [(i, i ^ bits) for i in range(voc_count)])

    def up(x, k):
        pairs = [(i, (i + k * stride) % voc_count) for i in range(voc_count)]
        return lax.ppermute(x, "voc", pairs) if k else x

    vrows, columns = weight.shape
    nblk = vrows // BLOCK
    lists = kept_blocks[:, 0, :].reshape(-1)
    counts = kept_counts[:, 0]
    frequent = jnp.any(counts > 1)
    meta = Meta(tok_count, nblk)
    m = jnp.concatenate([lists, counts, jnp.stack([tok_me, voc_me])]).astype(jnp.int32)

    tiles = gather_call(meta, m, weight.reshape(nblk, BLOCK, columns))
    pair = pair_call(hidden, flip(hidden, NC), tiles)
    pieces = [up(pair, k) for k in range(NZ)]
    w = exchange(tiles, frequent)
    pieces = [pair, *hold(pieces[1:], w)]
    others = [flip(piece, 1) for piece in pieces]

    near = logits_call(meta, m, pieces, w)
    logits, stats = logits_call(meta, m, others, w, near)
    stats = merge([up(stats, k) for k in range(NZ)])
    stats = [stats] + [flip(stats, bits) for bits in (1, NC, NC + 1)]
    grad_t, grad, other = other_call(
        meta, m, logits, stats, cotangent[None, :], targets[None, :], w
    )
    got = flip(other, 1)
    rows = rows_call(meta, m, grad_t, pieces, others)
    owed = mine_call(meta, m, grad, w, got, rows)
    parts = [up(part, k) for k, part in enumerate(owed)]
    returned = exchange(rows, frequent)
    keep, away = pick_call(meta, m, parts, returned)
    d_weight = combine_call(meta, m, returned)
    d_hidden = (keep + flip(away, NC).astype(F32)).astype(BF16)
    return (d_hidden, d_weight.reshape(vrows, columns))


def solution(mesh):
    placed = (
        P("tok", "voc"),
        P("voc", "tok"),
        P("tok"),
        P("tok"),
        P(None, "voc", None),
        P(None, "voc"),
    )
    return jax.shard_map(
        local,
        mesh=mesh,
        in_specs=placed,
        out_specs=(P("tok", "voc"), P("voc", "tok")),
        check_vma=False,
    )
```

```python
import functools

import jax
import jax.numpy as jnp
from jax import lax
from jax.experimental import pallas as pl
from jax.experimental.pallas import tpu as pltpu
from jax.sharding import PartitionSpec as P

BLOCK = 512
KMAX = 2
NEG = -1e30
F32 = jnp.float32
BF16 = jnp.bfloat16
VMEM_LIMIT = 16 * 1024 * 1024
VMEM = pl.BlockSpec(memory_space=pltpu.VMEM)
NZ, NY, NC = 4, 2, 2
NT = (((1,), (1,)), ((), ()))
NN = (((1,), (0,)), ((), ()))


def call(kernel, name, prefetch, grid, in_specs, out_specs, out_shape, scratch=(), flops=0, moved=0):
    return pl.pallas_call(
        kernel,
        grid_spec=pltpu.PrefetchScalarGridSpec(
            num_scalar_prefetch=prefetch,
            grid=grid,
            in_specs=in_specs,
            out_specs=out_specs,
            scratch_shapes=list(scratch),
        ),
        out_shape=out_shape,
        compiler_params=pltpu.CompilerParams(vmem_limit_bytes=VMEM_LIMIT),
        cost_estimate=pl.CostEstimate(flops=flops, bytes_accessed=moved, transcendentals=0),
        name=name,
    )


def dot(a, b, dims):
    return lax.dot_general(a, b, dims, preferred_element_type=F32)


class Meta:
    def __init__(self, tok_count, nblk):
        self.tok_count, self.nblk = tok_count, nblk

    def block(self, m, t, slot):
        return m[t * KMAX + slot]

    def kept(self, m, t):
        return m[self.tok_count * KMAX + t]

    def tok(self, m):
        return m[self.tok_count * (KMAX + 1)]

    def voc(self, m):
        return m[self.tok_count * (KMAX + 1) + 1]

    def core(self, m):
        return lax.rem(self.voc(m), NC)

    def y(self, m):
        return lax.rem(lax.div(self.voc(m), NC), NY)

    def count(self, m):
        return self.kept(m, self.tok(m))

    def start(self, m, slot):
        return (self.voc(m) * self.nblk + self.block(m, self.tok(m), slot)) * BLOCK

    def z(self, m):
        return lax.div(self.voc(m), NC * NY)

    def held(self, m, k, e):
        return lax.rem(self.z(m) + NZ - k, NZ) * NY + jnp.bitwise_xor(self.y(m), e)

    def owed(self, m, k, e):
        return lax.rem(self.z(m) + k, NZ) * NY + e


def gather_kernel(m, first, second, out):
    out[0, :BLOCK, :] = first[0]
    out[0, BLOCK:, :] = second[0]


def gather_call(meta, lists, weight):
    _, rows, columns = weight.shape
    shape = (meta.tok_count, KMAX * rows, columns)
    return call(
        gather_kernel,
        "gather",
        1,
        (meta.tok_count,),
        [
            pl.BlockSpec((1, rows, columns), lambda t, m, s=slot: (meta.block(m, t, s), 0, 0))
            for slot in range(KMAX)
        ],
        pl.BlockSpec((1, KMAX * rows, columns), lambda t, m: (t, 0, 0)),
        jax.ShapeDtypeStruct(shape, BF16),
        moved=4 * meta.tok_count * KMAX * rows * columns,
    )(lists, weight, weight)


def pair_kernel(hidden, near, tiles, out):
    del tiles
    out[0] = hidden[...]
    out[1] = near[...]


def pair_call(hidden, near, tiles):
    return call(
        pair_kernel,
        "pair",
        0,
        (),
        [VMEM, VMEM, pl.BlockSpec(memory_space=pl.ANY)],
        VMEM,
        jax.ShapeDtypeStruct((NY, *hidden.shape), hidden.dtype),
        moved=8 * hidden.size,
    )(hidden, near, tiles)


def hold(arrays, behind):
    n = len(arrays)
    anywhere = pl.BlockSpec(memory_space=pl.ANY)
    return pl.pallas_call(
        lambda *refs: None,
        in_specs=[anywhere] * (n + 1),
        out_specs=[anywhere] * n,
        out_shape=[jax.ShapeDtypeStruct(a.shape, a.dtype) for a in arrays],
        input_output_aliases={i: i for i in range(n)},
        compiler_params=pltpu.CompilerParams(vmem_limit_bytes=VMEM_LIMIT),
        name="hold",
    )(*arrays, behind)


def half_of(core, half):
    return pl.ds(pl.multiple_of(core * half, half), half)


def line_up(meta, m, pieces, w, slot, core, features, rows):
    half = pieces[0].shape[-1]
    for k, piece in enumerate(pieces):
        for e in range(NY):
            at = pl.ds((k * NY + e) * half, half)
            if slot == 0:
                features[:, at] = piece[e]
            rows[:, at] = w[meta.held(m, k, e), pl.ds(slot * BLOCK, BLOCK), half_of(core, half)]


def near_kernel(meta, m, p0, p1, p2, p3, w, logits, features, rows):
    for slot in range(KMAX):

        @pl.when(slot < meta.count(m))
        def _(slot=slot):
            line_up(meta, m, (p0, p1, p2, p3), w, slot, meta.core(m), features, rows)
            logits[pl.ds(slot * BLOCK, BLOCK), :] = dot(rows[...], features[...], NT)


def far_kernel(meta, m, p0, p1, p2, p3, w, near, logits, stats, features, rows):
    stats[0:1, :] = jnp.full(stats[0:1, :].shape, NEG, F32)
    stats[1:2, :] = jnp.zeros(stats[1:2, :].shape, F32)
    for slot in range(KMAX):

        @pl.when(slot < meta.count(m))
        def _(slot=slot):
            line_up(meta, m, (p0, p1, p2, p3), w, slot, 1 - meta.core(m), features, rows)
            some = pl.ds(slot * BLOCK, BLOCK)
            values = near[some, :] + dot(rows[...], features[...], NT)
            logits[some, :] = values
            old = stats[0:1, :]
            top = jnp.maximum(old, jnp.max(values, axis=0, keepdims=True))
            own = jnp.sum(jnp.exp(values - top), axis=0, keepdims=True)
            stats[1:2, :] = stats[1:2, :] * jnp.exp(old - top) + own
            stats[0:1, :] = top


def logits_call(meta, m, pieces, w, near=None):
    chunks, width, columns = w.shape
    _, tokens, half = pieces[0].shape
    shape = jax.ShapeDtypeStruct((width, tokens), F32)
    far = near is not None
    return call(
        functools.partial(far_kernel if far else near_kernel, meta),
        "logits_far" if far else "logits_near",
        1,
        (),
        [VMEM] * (NZ + 1 + far),
        [VMEM, VMEM] if far else VMEM,
        [shape, jax.ShapeDtypeStruct((2, tokens), F32)] if far else shape,
        [pltpu.VMEM((tokens, chunks * half), BF16), pltpu.VMEM((BLOCK, chunks * half), BF16)],
        flops=width * tokens * chunks * columns,
        moved=width * chunks * columns + 4 * width * tokens,
    )(m, *pieces, w, *[near] * far)


def other_kernel(meta, m, logits, s0, s1, s2, s3, cot, targets, w, grad_t, grad, other):
    count = meta.count(m)
    chunks, _, half = other.shape
    parts = [s0[...], s1[...], s2[...], s3[...]]
    top = functools.reduce(jnp.maximum, [s[0:1, :] for s in parts])
    lse = top + jnp.log(sum(s[1:2, :] * jnp.exp(s[0:1, :] - top) for s in parts))
    for slot in range(KMAX):
        rows = pl.ds(slot * BLOCK, BLOCK)

        @pl.when(slot < count)
        def _(slot=slot, rows=rows):
            prob = jnp.exp(logits[rows, :] - lse)
            place = lax.broadcasted_iota(jnp.int32, prob.shape, 0)
            hit = place == targets[...] - meta.start(m, slot)
            value = (cot[...] * (prob - jnp.where(hit, 1.0, 0.0))).astype(BF16)
            grad_t[rows, :] = value
            grad[:, rows] = value.T

    @pl.when(count == 0)
    def _():
        other[...] = jnp.zeros(other.shape, BF16)

    for n in range(1, KMAX + 1):

        @pl.when(count == n)
        def _(width=n * BLOCK):
            for c in range(chunks):
                rows = w[c, :width, half_of(1 - meta.core(m), half)]
                other[c] = dot(grad[:, :width], rows, NN).astype(BF16)


def other_call(meta, m, logits, stats, cot, targets, w):
    chunks, width, columns = w.shape
    tokens = logits.shape[1]
    return call(
        functools.partial(other_kernel, meta),
        "hidden_other",
        1,
        (),
        [VMEM] * 8,
        [VMEM] * 3,
        [
            jax.ShapeDtypeStruct((width, tokens), BF16),
            jax.ShapeDtypeStruct((tokens, width), BF16),
            jax.ShapeDtypeStruct((chunks, tokens, columns // NC), BF16),
        ],
        flops=width * tokens * chunks * columns,
        moved=w.size + 4 * logits.size,
    )(m, logits, *stats, cot, targets, w)


def rows_kernel(meta, m, grad_t, *refs):
    out = refs[-1]
    pieces, others = refs[:NZ], refs[NZ : 2 * NZ]
    half = pieces[0].shape[-1]
    core = meta.core(m)
    for n in range(1, KMAX + 1):

        @pl.when(meta.count(m) == n)
        def _(width=n * BLOCK):
            for k in range(NZ):
                for e in range(NY):
                    c = meta.held(m, k, e)
                    for side, piece in ((core, pieces[k]), (1 - core, others[k])):
                        value = dot(grad_t[:width, :], piece[e], NN)
                        out[c, :width, half_of(side, half)] = value.astype(BF16)


def rows_call(meta, m, grad_t, pieces, others):
    width, tokens = grad_t.shape
    half = pieces[0].shape[-1]
    chunks = NZ * NY
    return call(
        functools.partial(rows_kernel, meta),
        "head_rows",
        1,
        (),
        [VMEM] * (1 + 2 * NZ),
        VMEM,
        jax.ShapeDtypeStruct((chunks, width, NC * half), BF16),
        flops=2 * width * tokens * chunks * NC * half,
        moved=2 * chunks * width * NC * half,
    )(m, grad_t, *pieces, *others)


def mine_kernel(meta, m, grad, w, got, rows, *outs):
    del rows
    count = meta.count(m)
    half = got.shape[-1]
    for n in range(KMAX + 1):

        @pl.when(count == n)
        def _(width=n * BLOCK):
            for k, out in enumerate(outs):
                for e in range(NY):
                    c = meta.owed(m, k, e)
                    value = got[c].astype(F32)
                    if width:
                        own = w[c, :width, half_of(meta.core(m), half)]
                        value = value + dot(grad[:, :width], own, NN)
                    out[e] = value.astype(out.dtype)


def mine_call(meta, m, grad, w, got, rows):
    chunks, width, columns = w.shape
    tokens = grad.shape[0]
    shape = (NY, tokens, columns // NC)
    return call(
        functools.partial(mine_kernel, meta),
        "hidden_mine",
        1,
        (),
        [VMEM] * 3 + [pl.BlockSpec(memory_space=pl.ANY)],
        [VMEM] * NZ,
        [jax.ShapeDtypeStruct(shape, BF16 if k else F32) for k in range(NZ)],
        flops=width * tokens * chunks * columns,
        moved=w.size,
    )(m, grad, w, got, rows)


def combine_kernel(meta, m, pieces, out, total):
    block = pl.program_id(0)
    entries = [(t, slot) for t in range(meta.tok_count) for slot in range(KMAX)]
    here = [(meta.block(m, t, slot) == block) & (slot < meta.kept(m, t)) for t, slot in entries]
    number = sum(h.astype(jnp.int32) for h in here)

    def each(add):
        for (t, slot), found in zip(entries, here):

            @pl.when(found)
            def _(t=t, slot=slot):
                add(pieces[t, slot * BLOCK : (slot + 1) * BLOCK, :])

    def put(piece):
        out[0] = piece

    def accumulate(piece):
        total[...] += piece.astype(F32)

    @pl.when(number == 0)
    def _():
        out[0] = jnp.zeros(total.shape, BF16)

    @pl.when(number == 1)
    def _():
        each(put)

    @pl.when(number > 1)
    def _():
        total[...] = jnp.zeros(total.shape, F32)
        each(accumulate)
        out[0] = total[...].astype(BF16)


def combine_call(meta, m, pieces):
    columns = pieces.shape[2]
    return call(
        functools.partial(combine_kernel, meta),
        "combine",
        1,
        (meta.nblk,),
        [VMEM],
        pl.BlockSpec((1, BLOCK, columns), lambda b, m: (b, 0, 0)),
        jax.ShapeDtypeStruct((meta.nblk, BLOCK, columns), BF16),
        [pltpu.VMEM((BLOCK, columns), F32)],
        moved=2 * pieces.size + 2 * meta.nblk * BLOCK * columns,
    )(m, pieces)


def pick_kernel(meta, m, *refs):
    *parts, _, keep, away = refs
    y = meta.y(m)
    keep[...] = functools.reduce(jnp.add, [p[y].astype(F32) for p in parts])
    away[...] = functools.reduce(jnp.add, [p[1 - y].astype(F32) for p in parts]).astype(BF16)


def pick_call(meta, m, parts, returned):
    _, tokens, half = parts[0].shape
    return call(
        functools.partial(pick_kernel, meta),
        "pick",
        1,
        (),
        [VMEM] * len(parts) + [pl.BlockSpec(memory_space=pl.ANY)],
        [VMEM, VMEM],
        [
            jax.ShapeDtypeStruct((tokens, half), F32),
            jax.ShapeDtypeStruct((tokens, half), BF16),
        ],
        moved=12 * NY * tokens * half,
    )(m, *parts, returned)


def merge(parts):
    top = functools.reduce(jnp.maximum, [s[0] for s in parts])
    return jnp.stack([top, sum(s[1] * jnp.exp(s[0] - top) for s in parts)])


def exchange(parts, frequent):
    def swap(x):
        return lax.all_to_all(x, "tok", split_axis=0, concat_axis=0, tiled=True)

    def small(x):
        rest = jnp.zeros((x.shape[0], x.shape[1] - BLOCK, x.shape[2]), x.dtype)
        return jnp.concatenate([swap(x[:, :BLOCK]), rest], axis=1)

    return lax.cond(frequent, swap, small, parts)


def local(hidden, weight, targets, cotangent, kept_blocks, kept_counts):
    tok_count = lax.axis_size("tok")
    voc_count = lax.axis_size("voc")
    tok_me = lax.axis_index("tok")
    voc_me = lax.axis_index("voc")
    stride = NC * NY

    def flip(x, bits):
        return lax.ppermute(x, "voc", [(i, i ^ bits) for i in range(voc_count)])

    def up(x, k):
        pairs = [(i, (i + k * stride) % voc_count) for i in range(voc_count)]
        return lax.ppermute(x, "voc", pairs) if k else x

    vrows, columns = weight.shape
    nblk = vrows // BLOCK
    lists = kept_blocks[:, 0, :].reshape(-1)
    counts = kept_counts[:, 0]
    frequent = jnp.any(counts > 1)
    meta = Meta(tok_count, nblk)
    m = jnp.concatenate([lists, counts, jnp.stack([tok_me, voc_me])]).astype(jnp.int32)

    tiles = gather_call(meta, m, weight.reshape(nblk, BLOCK, columns))
    pair = pair_call(hidden, flip(hidden, NC), tiles)
    pieces = [up(pair, k) for k in range(NZ)]
    w = exchange(tiles, frequent)
    pieces = [pair, *hold(pieces[1:], w)]
    others = [flip(piece, 1) for piece in pieces]

    near = logits_call(meta, m, pieces, w)
    logits, stats = logits_call(meta, m, others, w, near)
    stats = merge([up(stats, k) for k in range(NZ)])
    stats = [stats] + [flip(stats, bits) for bits in (1, NC, NC + 1)]
    grad_t, grad, other = other_call(
        meta, m, logits, stats, cotangent[None, :], targets[None, :], w
    )
    got = flip(other, 1)
    rows = rows_call(meta, m, grad_t, pieces, others)
    owed = mine_call(meta, m, grad, w, got, rows)
    parts = [up(part, k) for k, part in enumerate(owed)]
    returned = exchange(rows, frequent)
    keep, away = pick_call(meta, m, parts, returned)
    d_weight = combine_call(meta, m, returned)
    d_hidden = (keep + flip(away, NC).astype(F32)).astype(BF16)
    return (d_hidden, d_weight.reshape(vrows, columns))


def solution(mesh):
    placed = (
        P("tok", "voc"),
        P("voc", "tok"),
        P("tok"),
        P("tok"),
        P(None, "voc", None),
        P(None, "voc"),
    )
    return jax.shard_map(
        local,
        mesh=mesh,
        in_specs=placed,
        out_specs=(P("tok", "voc"), P("voc", "tok")),
        check_vma=False,
    )
```

```python
import functools

import jax
import jax.numpy as jnp
from jax import lax
from jax.experimental import pallas as pl
from jax.experimental.pallas import tpu as pltpu
from jax.sharding import PartitionSpec as P

BLOCK = 512
KMAX = 2
NEG = -1e30
F32 = jnp.float32
BF16 = jnp.bfloat16
VMEM_LIMIT = 16 * 1024 * 1024
VMEM = pl.BlockSpec(memory_space=pltpu.VMEM)
NZ, NY, NC = 4, 2, 2
NT = (((1,), (1,)), ((), ()))
NN = (((1,), (0,)), ((), ()))


def call(kernel, name, prefetch, grid, in_specs, out_specs, out_shape, scratch=(), flops=0, moved=0):
    return pl.pallas_call(
        kernel,
        grid_spec=pltpu.PrefetchScalarGridSpec(
            num_scalar_prefetch=prefetch,
            grid=grid,
            in_specs=in_specs,
            out_specs=out_specs,
            scratch_shapes=list(scratch),
        ),
        out_shape=out_shape,
        compiler_params=pltpu.CompilerParams(vmem_limit_bytes=VMEM_LIMIT),
        cost_estimate=pl.CostEstimate(flops=flops, bytes_accessed=moved, transcendentals=0),
        name=name,
    )


def dot(a, b, dims):
    return lax.dot_general(a, b, dims, preferred_element_type=F32)


class Meta:
    def __init__(self, tok_count, nblk):
        self.tok_count, self.nblk = tok_count, nblk

    def block(self, m, t, slot):
        return m[t * KMAX + slot]

    def kept(self, m, t):
        return m[self.tok_count * KMAX + t]

    def tok(self, m):
        return m[self.tok_count * (KMAX + 1)]

    def voc(self, m):
        return m[self.tok_count * (KMAX + 1) + 1]

    def core(self, m):
        return lax.rem(self.voc(m), NC)

    def y(self, m):
        return lax.rem(lax.div(self.voc(m), NC), NY)

    def count(self, m):
        return self.kept(m, self.tok(m))

    def start(self, m, slot):
        return (self.voc(m) * self.nblk + self.block(m, self.tok(m), slot)) * BLOCK

    def z(self, m):
        return lax.div(self.voc(m), NC * NY)

    def held(self, m, k, e):
        return lax.rem(self.z(m) + NZ - k, NZ) * NY + jnp.bitwise_xor(self.y(m), e)

    def owed(self, m, k, e):
        return lax.rem(self.z(m) + k, NZ) * NY + e


def gather_kernel(m, first, second, out):
    out[0, :BLOCK, :] = first[0]
    out[0, BLOCK:, :] = second[0]


def gather_call(meta, lists, weight):
    _, rows, columns = weight.shape
    shape = (meta.tok_count, KMAX * rows, columns)
    return call(
        gather_kernel,
        "gather",
        1,
        (meta.tok_count,),
        [
            pl.BlockSpec((1, rows, columns), lambda t, m, s=slot: (meta.block(m, t, s), 0, 0))
            for slot in range(KMAX)
        ],
        pl.BlockSpec((1, KMAX * rows, columns), lambda t, m: (t, 0, 0)),
        jax.ShapeDtypeStruct(shape, BF16),
        moved=4 * meta.tok_count * KMAX * rows * columns,
    )(lists, weight, weight)


def pair_kernel(hidden, near, tiles, out):
    del tiles
    out[0] = hidden[...]
    out[1] = near[...]


def pair_call(hidden, near, tiles):
    return call(
        pair_kernel,
        "pair",
        0,
        (),
        [VMEM, VMEM, pl.BlockSpec(memory_space=pl.ANY)],
        VMEM,
        jax.ShapeDtypeStruct((NY, *hidden.shape), hidden.dtype),
        moved=8 * hidden.size,
    )(hidden, near, tiles)


def hold(arrays, behind):
    n = len(arrays)
    anywhere = pl.BlockSpec(memory_space=pl.ANY)
    return pl.pallas_call(
        lambda *refs: None,
        in_specs=[anywhere] * (n + 1),
        out_specs=[anywhere] * n,
        out_shape=[jax.ShapeDtypeStruct(a.shape, a.dtype) for a in arrays],
        input_output_aliases={i: i for i in range(n)},
        compiler_params=pltpu.CompilerParams(vmem_limit_bytes=VMEM_LIMIT),
        name="hold",
    )(*arrays, behind)


def half_of(core, half):
    return pl.ds(pl.multiple_of(core * half, half), half)


def line_up(meta, m, pieces, w, slot, core, features, rows):
    half = pieces[0].shape[-1]
    for k, piece in enumerate(pieces):
        for e in range(NY):
            at = pl.ds((k * NY + e) * half, half)
            if slot == 0:
                features[:, at] = piece[e]
            rows[:, at] = w[meta.held(m, k, e), pl.ds(slot * BLOCK, BLOCK), half_of(core, half)]


def near_kernel(meta, m, p0, p1, p2, p3, w, logits, features, rows):
    for slot in range(KMAX):

        @pl.when(slot < meta.count(m))
        def _(slot=slot):
            line_up(meta, m, (p0, p1, p2, p3), w, slot, meta.core(m), features, rows)
            logits[pl.ds(slot * BLOCK, BLOCK), :] = dot(rows[...], features[...], NT)


def far_kernel(meta, m, p0, p1, p2, p3, w, near, logits, stats, features, rows):
    stats[0:1, :] = jnp.full(stats[0:1, :].shape, NEG, F32)
    stats[1:2, :] = jnp.zeros(stats[1:2, :].shape, F32)
    for slot in range(KMAX):

        @pl.when(slot < meta.count(m))
        def _(slot=slot):
            line_up(meta, m, (p0, p1, p2, p3), w, slot, 1 - meta.core(m), features, rows)
            some = pl.ds(slot * BLOCK, BLOCK)
            values = near[some, :] + dot(rows[...], features[...], NT)
            logits[some, :] = values
            old = stats[0:1, :]
            top = jnp.maximum(old, jnp.max(values, axis=0, keepdims=True))
            own = jnp.sum(jnp.exp(values - top), axis=0, keepdims=True)
            stats[1:2, :] = stats[1:2, :] * jnp.exp(old - top) + own
            stats[0:1, :] = top


def logits_call(meta, m, pieces, w, near=None):
    chunks, width, columns = w.shape
    _, tokens, half = pieces[0].shape
    shape = jax.ShapeDtypeStruct((width, tokens), F32)
    far = near is not None
    return call(
        functools.partial(far_kernel if far else near_kernel, meta),
        "logits_far" if far else "logits_near",
        1,
        (),
        [VMEM] * (NZ + 1 + far),
        [VMEM, VMEM] if far else VMEM,
        [shape, jax.ShapeDtypeStruct((2, tokens), F32)] if far else shape,
        [pltpu.VMEM((tokens, chunks * half), BF16), pltpu.VMEM((BLOCK, chunks * half), BF16)],
        flops=width * tokens * chunks * columns,
        moved=width * chunks * columns + 4 * width * tokens,
    )(m, *pieces, w, *[near] * far)


def other_kernel(meta, m, logits, s0, s1, s2, s3, cot, targets, w, grad_t, grad, other):
    count = meta.count(m)
    chunks, _, half = other.shape
    parts = [s0[...], s1[...], s2[...], s3[...]]
    top = functools.reduce(jnp.maximum, [s[0:1, :] for s in parts])
    lse = top + jnp.log(sum(s[1:2, :] * jnp.exp(s[0:1, :] - top) for s in parts))
    for slot in range(KMAX):
        rows = pl.ds(slot * BLOCK, BLOCK)

        @pl.when(slot < count)
        def _(slot=slot, rows=rows):
            prob = jnp.exp(logits[rows, :] - lse)
            place = lax.broadcasted_iota(jnp.int32, prob.shape, 0)
            hit = place == targets[...] - meta.start(m, slot)
            value = (cot[...] * (prob - jnp.where(hit, 1.0, 0.0))).astype(BF16)
            grad_t[rows, :] = value
            grad[:, rows] = value.T

    @pl.when(count == 0)
    def _():
        other[...] = jnp.zeros(other.shape, BF16)

    for n in range(1, KMAX + 1):

        @pl.when(count == n)
        def _(width=n * BLOCK):
            for c in range(chunks):
                rows = w[c, :width, half_of(1 - meta.core(m), half)]
                other[c] = dot(grad[:, :width], rows, NN).astype(BF16)


def other_call(meta, m, logits, stats, cot, targets, w):
    chunks, width, columns = w.shape
    tokens = logits.shape[1]
    return call(
        functools.partial(other_kernel, meta),
        "hidden_other",
        1,
        (),
        [VMEM] * 8,
        [VMEM] * 3,
        [
            jax.ShapeDtypeStruct((width, tokens), BF16),
            jax.ShapeDtypeStruct((tokens, width), BF16),
            jax.ShapeDtypeStruct((chunks, tokens, columns // NC), BF16),
        ],
        flops=width * tokens * chunks * columns,
        moved=w.size + 4 * logits.size,
    )(m, logits, *stats, cot, targets, w)


def rows_kernel(meta, m, grad_t, *refs):
    out = refs[-1]
    pieces, others = refs[:NZ], refs[NZ : 2 * NZ]
    half = pieces[0].shape[-1]
    core = meta.core(m)
    for n in range(1, KMAX + 1):

        @pl.when(meta.count(m) == n)
        def _(width=n * BLOCK):
            for k in range(NZ):
                for e in range(NY):
                    c = meta.held(m, k, e)
                    for side, piece in ((core, pieces[k]), (1 - core, others[k])):
                        value = dot(grad_t[:width, :], piece[e], NN)
                        out[c, :width, half_of(side, half)] = value.astype(BF16)


def rows_call(meta, m, grad_t, pieces, others):
    width, tokens = grad_t.shape
    half = pieces[0].shape[-1]
    chunks = NZ * NY
    return call(
        functools.partial(rows_kernel, meta),
        "head_rows",
        1,
        (),
        [VMEM] * (1 + 2 * NZ),
        VMEM,
        jax.ShapeDtypeStruct((chunks, width, NC * half), BF16),
        flops=2 * width * tokens * chunks * NC * half,
        moved=2 * chunks * width * NC * half,
    )(m, grad_t, *pieces, *others)


def mine_kernel(meta, m, grad, w, got, rows, *outs):
    del rows
    count = meta.count(m)
    half = got.shape[-1]
    for n in range(KMAX + 1):

        @pl.when(count == n)
        def _(width=n * BLOCK):
            for k, out in enumerate(outs):
                for e in range(NY):
                    c = meta.owed(m, k, e)
                    value = got[c].astype(F32)
                    if width:
                        own = w[c, :width, half_of(meta.core(m), half)]
                        value = value + dot(grad[:, :width], own, NN)
                    out[e] = value.astype(out.dtype)


def mine_call(meta, m, grad, w, got, rows):
    chunks, width, columns = w.shape
    tokens = grad.shape[0]
    shape = (NY, tokens, columns // NC)
    return call(
        functools.partial(mine_kernel, meta),
        "hidden_mine",
        1,
        (),
        [VMEM] * 3 + [pl.BlockSpec(memory_space=pl.ANY)],
        [VMEM] * NZ,
        [jax.ShapeDtypeStruct(shape, BF16 if k else F32) for k in range(NZ)],
        flops=width * tokens * chunks * columns,
        moved=w.size,
    )(m, grad, w, got, rows)


def combine_kernel(meta, m, pieces, out, total):
    block = pl.program_id(0)
    entries = [(t, slot) for t in range(meta.tok_count) for slot in range(KMAX)]
    here = [(meta.block(m, t, slot) == block) & (slot < meta.kept(m, t)) for t, slot in entries]
    number = sum(h.astype(jnp.int32) for h in here)
    first = functools.reduce(
        jnp.minimum, [jnp.where(h, i, len(entries) - 1) for i, h in enumerate(here)]
    )
    last = functools.reduce(jnp.maximum, [jnp.where(h, i, 0) for i, h in enumerate(here)])

    def piece(i):
        rows = pl.ds(pl.multiple_of(lax.rem(i, KMAX) * BLOCK, BLOCK), BLOCK)
        return pieces[lax.div(i, KMAX), rows, :]

    @pl.when(number == 0)
    def _():
        out[0] = jnp.zeros(total.shape, BF16)

    @pl.when(number == 1)
    def _():
        out[0] = piece(first)

    @pl.when(number == 2)
    def _():
        out[0] = (piece(first).astype(F32) + piece(last).astype(F32)).astype(BF16)

    @pl.when(number > 2)
    def _():
        total[...] = piece(first).astype(F32) + piece(last).astype(F32)
        for i, ((t, slot), found) in enumerate(zip(entries, here)):

            @pl.when(found & (i != first) & (i != last))
            def _(t=t, slot=slot):
                total[...] += pieces[t, slot * BLOCK : (slot + 1) * BLOCK, :].astype(F32)

        out[0] = total[...].astype(BF16)


def combine_call(meta, m, pieces):
    columns = pieces.shape[2]
    return call(
        functools.partial(combine_kernel, meta),
        "combine",
        1,
        (meta.nblk,),
        [VMEM],
        pl.BlockSpec((1, BLOCK, columns), lambda b, m: (b, 0, 0)),
        jax.ShapeDtypeStruct((meta.nblk, BLOCK, columns), BF16),
        [pltpu.VMEM((BLOCK, columns), F32)],
        moved=2 * pieces.size + 2 * meta.nblk * BLOCK * columns,
    )(m, pieces)


def pick_kernel(meta, m, *refs):
    *parts, _, keep, away = refs
    y = meta.y(m)
    keep[...] = functools.reduce(jnp.add, [p[y].astype(F32) for p in parts])
    away[...] = functools.reduce(jnp.add, [p[1 - y].astype(F32) for p in parts]).astype(BF16)


def pick_call(meta, m, parts, returned):
    _, tokens, half = parts[0].shape
    return call(
        functools.partial(pick_kernel, meta),
        "pick",
        1,
        (),
        [VMEM] * len(parts) + [pl.BlockSpec(memory_space=pl.ANY)],
        [VMEM, VMEM],
        [
            jax.ShapeDtypeStruct((tokens, half), F32),
            jax.ShapeDtypeStruct((tokens, half), BF16),
        ],
        moved=12 * NY * tokens * half,
    )(m, *parts, returned)


def merge(parts):
    top = functools.reduce(jnp.maximum, [s[0] for s in parts])
    return jnp.stack([top, sum(s[1] * jnp.exp(s[0] - top) for s in parts)])


def exchange(parts, frequent):
    def swap(x):
        return lax.all_to_all(x, "tok", split_axis=0, concat_axis=0, tiled=True)

    def small(x):
        rest = jnp.zeros((x.shape[0], x.shape[1] - BLOCK, x.shape[2]), x.dtype)
        return jnp.concatenate([swap(x[:, :BLOCK]), rest], axis=1)

    return lax.cond(frequent, swap, small, parts)


def local(hidden, weight, targets, cotangent, kept_blocks, kept_counts):
    tok_count = lax.axis_size("tok")
    voc_count = lax.axis_size("voc")
    tok_me = lax.axis_index("tok")
    voc_me = lax.axis_index("voc")
    stride = NC * NY

    def flip(x, bits):
        return lax.ppermute(x, "voc", [(i, i ^ bits) for i in range(voc_count)])

    def up(x, k):
        pairs = [(i, (i + k * stride) % voc_count) for i in range(voc_count)]
        return lax.ppermute(x, "voc", pairs) if k else x

    vrows, columns = weight.shape
    nblk = vrows // BLOCK
    lists = kept_blocks[:, 0, :].reshape(-1)
    counts = kept_counts[:, 0]
    frequent = jnp.any(counts > 1)
    meta = Meta(tok_count, nblk)
    m = jnp.concatenate([lists, counts, jnp.stack([tok_me, voc_me])]).astype(jnp.int32)

    tiles = gather_call(meta, m, weight.reshape(nblk, BLOCK, columns))
    pair = pair_call(hidden, flip(hidden, NC), tiles)
    pieces = [up(pair, k) for k in range(NZ)]
    w = exchange(tiles, frequent)
    pieces = [pair, *hold(pieces[1:], w)]
    others = [flip(piece, 1) for piece in pieces]

    near = logits_call(meta, m, pieces, w)
    logits, stats = logits_call(meta, m, others, w, near)
    stats = merge([up(stats, k) for k in range(NZ)])
    stats = [stats] + [flip(stats, bits) for bits in (1, NC, NC + 1)]
    grad_t, grad, other = other_call(
        meta, m, logits, stats, cotangent[None, :], targets[None, :], w
    )
    got = flip(other, 1)
    rows = rows_call(meta, m, grad_t, pieces, others)
    owed = mine_call(meta, m, grad, w, got, rows)
    parts = [up(part, k) for k, part in enumerate(owed)]
    returned = exchange(rows, frequent)
    keep, away = pick_call(meta, m, parts, returned)
    d_weight = combine_call(meta, m, returned)
    d_hidden = (keep + flip(away, NC).astype(F32)).astype(BF16)
    return (d_hidden, d_weight.reshape(vrows, columns))


def solution(mesh):
    placed = (
        P("tok", "voc"),
        P("voc", "tok"),
        P("tok"),
        P("tok"),
        P(None, "voc", None),
        P(None, "voc"),
    )
    return jax.shard_map(
        local,
        mesh=mesh,
        in_specs=placed,
        out_specs=(P("tok", "voc"), P("voc", "tok")),
        check_vma=False,
    )
```

```python
import functools

import jax
import jax.numpy as jnp
from jax import lax
from jax.experimental import pallas as pl
from jax.experimental.pallas import tpu as pltpu
from jax.sharding import PartitionSpec as P

BLOCK = 512
KMAX = 2
NEG = -1e30
F32 = jnp.float32
BF16 = jnp.bfloat16
VMEM_LIMIT = 16 * 1024 * 1024
VMEM = pl.BlockSpec(memory_space=pltpu.VMEM)
NZ, NY, NC = 4, 2, 2
NT = (((1,), (1,)), ((), ()))
NN = (((1,), (0,)), ((), ()))


def call(kernel, name, prefetch, grid, in_specs, out_specs, out_shape, scratch=(), flops=0, moved=0):
    return pl.pallas_call(
        kernel,
        grid_spec=pltpu.PrefetchScalarGridSpec(
            num_scalar_prefetch=prefetch,
            grid=grid,
            in_specs=in_specs,
            out_specs=out_specs,
            scratch_shapes=list(scratch),
        ),
        out_shape=out_shape,
        compiler_params=pltpu.CompilerParams(vmem_limit_bytes=VMEM_LIMIT),
        cost_estimate=pl.CostEstimate(flops=flops, bytes_accessed=moved, transcendentals=0),
        name=name,
    )


def dot(a, b, dims):
    return lax.dot_general(a, b, dims, preferred_element_type=F32)


class Meta:
    def __init__(self, tok_count, nblk):
        self.tok_count, self.nblk = tok_count, nblk

    def block(self, m, t, slot):
        return m[t * KMAX + slot]

    def kept(self, m, t):
        return m[self.tok_count * KMAX + t]

    def tok(self, m):
        return m[self.tok_count * (KMAX + 1)]

    def voc(self, m):
        return m[self.tok_count * (KMAX + 1) + 1]

    def core(self, m):
        return lax.rem(self.voc(m), NC)

    def y(self, m):
        return lax.rem(lax.div(self.voc(m), NC), NY)

    def count(self, m):
        return self.kept(m, self.tok(m))

    def start(self, m, slot):
        return (self.voc(m) * self.nblk + self.block(m, self.tok(m), slot)) * BLOCK

    def z(self, m):
        return lax.div(self.voc(m), NC * NY)

    def held(self, m, k, e):
        return lax.rem(self.z(m) + NZ - k, NZ) * NY + jnp.bitwise_xor(self.y(m), e)

    def owed(self, m, k, e):
        return lax.rem(self.z(m) + k, NZ) * NY + e


def gather_kernel(m, first, second, out):
    out[0, :BLOCK, :] = first[0]
    out[0, BLOCK:, :] = second[0]


def gather_call(meta, lists, weight):
    _, rows, columns = weight.shape
    shape = (meta.tok_count, KMAX * rows, columns)
    return call(
        gather_kernel,
        "gather",
        1,
        (meta.tok_count,),
        [
            pl.BlockSpec((1, rows, columns), lambda t, m, s=slot: (meta.block(m, t, s), 0, 0))
            for slot in range(KMAX)
        ],
        pl.BlockSpec((1, KMAX * rows, columns), lambda t, m: (t, 0, 0)),
        jax.ShapeDtypeStruct(shape, BF16),
        moved=4 * meta.tok_count * KMAX * rows * columns,
    )(lists, weight, weight)


def pair_kernel(hidden, near, tiles, frequent, out):
    del tiles, frequent
    out[0] = hidden[...]
    out[1] = near[...]


def pair_call(hidden, near, *behind):
    return call(
        pair_kernel,
        "pair",
        0,
        (),
        [VMEM, VMEM] + [pl.BlockSpec(memory_space=pl.ANY)] * len(behind),
        VMEM,
        jax.ShapeDtypeStruct((NY, *hidden.shape), hidden.dtype),
        moved=8 * hidden.size,
    )(hidden, near, *behind)


def hold(arrays, behind):
    n = len(arrays)
    anywhere = pl.BlockSpec(memory_space=pl.ANY)
    return pl.pallas_call(
        lambda *refs: None,
        in_specs=[anywhere] * (n + 1),
        out_specs=[anywhere] * n,
        out_shape=[jax.ShapeDtypeStruct(a.shape, a.dtype) for a in arrays],
        input_output_aliases={i: i for i in range(n)},
        compiler_params=pltpu.CompilerParams(vmem_limit_bytes=VMEM_LIMIT),
        name="hold",
    )(*arrays, behind)


def half_of(core, half):
    return pl.ds(pl.multiple_of(core * half, half), half)


def products(meta, m, pieces, w, core, features, rows, slots):
    half = pieces[0].shape[-1]
    places = [(k, e) for k in range(NZ) for e in range(NY)]
    for i, (k, e) in enumerate(places):
        features[:, i * half : (i + 1) * half] = pieces[k][e]
    for slot in range(slots):
        some = pl.ds(slot * BLOCK, BLOCK)
        for i, (k, e) in enumerate(places):
            rows[slot, :, i * half : (i + 1) * half] = w[meta.held(m, k, e), some, half_of(core, half)]
    return [dot(rows[slot], features[...], NT) for slot in range(slots)]


def near_kernel(meta, m, p0, p1, p2, p3, w, logits, features, rows):
    for n in range(1, KMAX + 1):

        @pl.when(meta.count(m) == n)
        def _(n=n):
            found = products(meta, m, (p0, p1, p2, p3), w, meta.core(m), features, rows, n)
            for slot, values in enumerate(found):
                logits[pl.ds(slot * BLOCK, BLOCK), :] = values


def far_kernel(meta, m, p0, p1, p2, p3, w, near, logits, stats, features, rows):
    @pl.when(meta.count(m) == 0)
    def _():
        stats[0:1, :] = jnp.full(stats[0:1, :].shape, NEG, F32)
        stats[1:2, :] = jnp.zeros(stats[1:2, :].shape, F32)

    for n in range(1, KMAX + 1):

        @pl.when(meta.count(m) == n)
        def _(n=n):
            found = products(meta, m, (p0, p1, p2, p3), w, 1 - meta.core(m), features, rows, n)
            tops, sums = [], []
            for slot, values in enumerate(found):
                some = pl.ds(slot * BLOCK, BLOCK)
                values = near[some, :] + values
                logits[some, :] = values
                tops.append(jnp.max(values, axis=0, keepdims=True))
                sums.append(jnp.sum(jnp.exp(values - tops[-1]), axis=0, keepdims=True))
            top = functools.reduce(jnp.maximum, tops)
            stats[0:1, :] = top
            stats[1:2, :] = sum(s * jnp.exp(t - top) for s, t in zip(sums, tops))


def logits_call(meta, m, pieces, w, near=None):
    chunks, width, columns = w.shape
    _, tokens, half = pieces[0].shape
    shape = jax.ShapeDtypeStruct((width, tokens), F32)
    far = near is not None
    return call(
        functools.partial(far_kernel if far else near_kernel, meta),
        "logits_far" if far else "logits_near",
        1,
        (),
        [VMEM] * (NZ + 1 + far),
        [VMEM, VMEM] if far else VMEM,
        [shape, jax.ShapeDtypeStruct((2, tokens), F32)] if far else shape,
        [
            pltpu.VMEM((tokens, chunks * half), BF16),
            pltpu.VMEM((KMAX, BLOCK, chunks * half), BF16),
        ],
        flops=width * tokens * chunks * columns,
        moved=width * chunks * columns + 4 * width * tokens,
    )(m, *pieces, w, *[near] * far)


def other_kernel(meta, m, logits, s0, s1, s2, s3, cot, targets, w, grad_t, grad, other):
    count = meta.count(m)
    chunks, _, half = other.shape
    parts = [s0[...], s1[...], s2[...], s3[...]]
    top = functools.reduce(jnp.maximum, [s[0:1, :] for s in parts])
    lse = top + jnp.log(sum(s[1:2, :] * jnp.exp(s[0:1, :] - top) for s in parts))
    for slot in range(KMAX):
        rows = pl.ds(slot * BLOCK, BLOCK)

        @pl.when(slot < count)
        def _(slot=slot, rows=rows):
            prob = jnp.exp(logits[rows, :] - lse)
            place = lax.broadcasted_iota(jnp.int32, prob.shape, 0)
            hit = place == targets[...] - meta.start(m, slot)
            value = (cot[...] * (prob - jnp.where(hit, 1.0, 0.0))).astype(BF16)
            grad_t[rows, :] = value
            grad[:, rows] = value.T

    @pl.when(count == 0)
    def _():
        other[...] = jnp.zeros(other.shape, BF16)

    for n in range(1, KMAX + 1):

        @pl.when(count == n)
        def _(width=n * BLOCK):
            for c in range(chunks):
                rows = w[c, :width, half_of(1 - meta.core(m), half)]
                other[c] = dot(grad[:, :width], rows, NN).astype(BF16)


def other_call(meta, m, logits, stats, cot, targets, w):
    chunks, width, columns = w.shape
    tokens = logits.shape[1]
    return call(
        functools.partial(other_kernel, meta),
        "hidden_other",
        1,
        (),
        [VMEM] * 8,
        [VMEM] * 3,
        [
            jax.ShapeDtypeStruct((width, tokens), BF16),
            jax.ShapeDtypeStruct((tokens, width), BF16),
            jax.ShapeDtypeStruct((chunks, tokens, columns // NC), BF16),
        ],
        flops=width * tokens * chunks * columns,
        moved=w.size + 4 * logits.size,
    )(m, logits, *stats, cot, targets, w)


def rows_kernel(meta, m, grad_t, *refs):
    out = refs[-1]
    pieces, others = refs[:NZ], refs[NZ : 2 * NZ]
    half = pieces[0].shape[-1]
    core = meta.core(m)
    for n in range(1, KMAX + 1):

        @pl.when(meta.count(m) == n)
        def _(width=n * BLOCK):
            for k in range(NZ):
                for e in range(NY):
                    c = meta.held(m, k, e)
                    for side, piece in ((core, pieces[k]), (1 - core, others[k])):
                        value = dot(grad_t[:width, :], piece[e], NN)
                        out[c, :width, half_of(side, half)] = value.astype(BF16)


def rows_call(meta, m, grad_t, pieces, others):
    width, tokens = grad_t.shape
    half = pieces[0].shape[-1]
    chunks = NZ * NY
    return call(
        functools.partial(rows_kernel, meta),
        "head_rows",
        1,
        (),
        [VMEM] * (1 + 2 * NZ),
        VMEM,
        jax.ShapeDtypeStruct((chunks, width, NC * half), BF16),
        flops=2 * width * tokens * chunks * NC * half,
        moved=2 * chunks * width * NC * half,
    )(m, grad_t, *pieces, *others)


def mine_kernel(meta, m, grad, w, got, rows, *outs):
    del rows
    count = meta.count(m)
    half = got.shape[-1]
    for n in range(KMAX + 1):

        @pl.when(count == n)
        def _(width=n * BLOCK):
            for k, out in enumerate(outs):
                for e in range(NY):
                    c = meta.owed(m, k, e)
                    value = got[c].astype(F32)
                    if width:
                        own = w[c, :width, half_of(meta.core(m), half)]
                        value = value + dot(grad[:, :width], own, NN)
                    out[e] = value.astype(out.dtype)


def mine_call(meta, m, grad, w, got, rows):
    chunks, width, columns = w.shape
    tokens = grad.shape[0]
    shape = (NY, tokens, columns // NC)
    return call(
        functools.partial(mine_kernel, meta),
        "hidden_mine",
        1,
        (),
        [VMEM] * 3 + [pl.BlockSpec(memory_space=pl.ANY)],
        [VMEM] * NZ,
        [jax.ShapeDtypeStruct(shape, BF16 if k else F32) for k in range(NZ)],
        flops=width * tokens * chunks * columns,
        moved=w.size,
    )(m, grad, w, got, rows)


def combine_kernel(meta, m, pieces, out, total):
    block = pl.program_id(0)
    entries = [(t, slot) for t in range(meta.tok_count) for slot in range(KMAX)]
    here = [(meta.block(m, t, slot) == block) & (slot < meta.kept(m, t)) for t, slot in entries]
    number = sum(h.astype(jnp.int32) for h in here)
    first = functools.reduce(
        jnp.minimum, [jnp.where(h, i, len(entries) - 1) for i, h in enumerate(here)]
    )
    last = functools.reduce(jnp.maximum, [jnp.where(h, i, 0) for i, h in enumerate(here)])

    def piece(i):
        rows = pl.ds(pl.multiple_of(lax.rem(i, KMAX) * BLOCK, BLOCK), BLOCK)
        return pieces[lax.div(i, KMAX), rows, :]

    @pl.when(number == 0)
    def _():
        out[0] = jnp.zeros(total.shape, BF16)

    @pl.when(number == 1)
    def _():
        out[0] = piece(first)

    @pl.when(number == 2)
    def _():
        out[0] = (piece(first).astype(F32) + piece(last).astype(F32)).astype(BF16)

    @pl.when(number > 2)
    def _():
        total[...] = piece(first).astype(F32) + piece(last).astype(F32)
        for i, ((t, slot), found) in enumerate(zip(entries, here)):

            @pl.when(found & (i != first) & (i != last))
            def _(t=t, slot=slot):
                total[...] += pieces[t, slot * BLOCK : (slot + 1) * BLOCK, :].astype(F32)

        out[0] = total[...].astype(BF16)


def combine_call(meta, m, pieces):
    columns = pieces.shape[2]
    return call(
        functools.partial(combine_kernel, meta),
        "combine",
        1,
        (meta.nblk,),
        [VMEM],
        pl.BlockSpec((1, BLOCK, columns), lambda b, m: (b, 0, 0)),
        jax.ShapeDtypeStruct((meta.nblk, BLOCK, columns), BF16),
        [pltpu.VMEM((BLOCK, columns), F32)],
        moved=2 * pieces.size + 2 * meta.nblk * BLOCK * columns,
    )(m, pieces)


def pick_kernel(meta, m, *refs):
    *parts, _, keep, away = refs
    y = meta.y(m)
    keep[...] = functools.reduce(jnp.add, [p[y].astype(F32) for p in parts])
    away[...] = functools.reduce(jnp.add, [p[1 - y].astype(F32) for p in parts]).astype(BF16)


def pick_call(meta, m, parts, returned):
    _, tokens, half = parts[0].shape
    return call(
        functools.partial(pick_kernel, meta),
        "pick",
        1,
        (),
        [VMEM] * len(parts) + [pl.BlockSpec(memory_space=pl.ANY)],
        [VMEM, VMEM],
        [
            jax.ShapeDtypeStruct((tokens, half), F32),
            jax.ShapeDtypeStruct((tokens, half), BF16),
        ],
        moved=12 * NY * tokens * half,
    )(m, *parts, returned)


def merge(parts):
    top = functools.reduce(jnp.maximum, [s[0] for s in parts])
    return jnp.stack([top, sum(s[1] * jnp.exp(s[0] - top) for s in parts)])


def exchange(parts, frequent):
    def swap(x):
        return lax.all_to_all(x, "tok", split_axis=0, concat_axis=0, tiled=True)

    def small(x):
        rest = jnp.zeros((x.shape[0], x.shape[1] - BLOCK, x.shape[2]), x.dtype)
        return jnp.concatenate([swap(x[:, :BLOCK]), rest], axis=1)

    return lax.cond(frequent[0, 0] > 1, swap, small, parts)


def local(hidden, weight, targets, cotangent, kept_blocks, kept_counts):
    tok_count = lax.axis_size("tok")
    voc_count = lax.axis_size("voc")
    tok_me = lax.axis_index("tok")
    voc_me = lax.axis_index("voc")
    stride = NC * NY

    def flip(x, bits):
        return lax.ppermute(x, "voc", [(i, i ^ bits) for i in range(voc_count)])

    def up(x, k):
        pairs = [(i, (i + k * stride) % voc_count) for i in range(voc_count)]
        return lax.ppermute(x, "voc", pairs) if k else x

    vrows, columns = weight.shape
    nblk = vrows // BLOCK
    lists = kept_blocks[:, 0, :].reshape(-1)
    counts = kept_counts[:, 0]
    frequent = jnp.max(counts)[None, None]
    meta = Meta(tok_count, nblk)
    m = jnp.concatenate([lists, counts, jnp.stack([tok_me, voc_me])]).astype(jnp.int32)

    tiles = gather_call(meta, m, weight.reshape(nblk, BLOCK, columns))
    pair = pair_call(hidden, flip(hidden, NC), tiles, frequent)
    pieces = [up(pair, k) for k in range(NZ)]
    w = exchange(tiles, frequent)
    pieces = [pair, *hold(pieces[1:], w)]
    others = [flip(piece, 1) for piece in pieces]

    near = logits_call(meta, m, pieces, w)
    logits, stats = logits_call(meta, m, others, w, near)
    stats = merge([up(stats, k) for k in range(NZ)])
    stats = [stats] + [flip(stats, bits) for bits in (1, NC, NC + 1)]
    grad_t, grad, other = other_call(
        meta, m, logits, stats, cotangent[None, :], targets[None, :], w
    )
    got = flip(other, 1)
    rows = rows_call(meta, m, grad_t, pieces, others)
    owed = mine_call(meta, m, grad, w, got, rows)
    parts = [up(part, k) for k, part in enumerate(owed)]
    returned = exchange(rows, frequent)
    keep, away = pick_call(meta, m, parts, returned)
    d_weight = combine_call(meta, m, returned)
    d_hidden = (keep + flip(away, NC).astype(F32)).astype(BF16)
    return (d_hidden, d_weight.reshape(vrows, columns))


def solution(mesh):
    placed = (
        P("tok", "voc"),
        P("voc", "tok"),
        P("tok"),
        P("tok"),
        P(None, "voc", None),
        P(None, "voc"),
    )
    return jax.shard_map(
        local,
        mesh=mesh,
        in_specs=placed,
        out_specs=(P("tok", "voc"), P("voc", "tok")),
        check_vma=False,
    )
```

```python
import functools

import jax
import jax.numpy as jnp
from jax import lax
from jax.experimental import pallas as pl
from jax.experimental.pallas import tpu as pltpu
from jax.sharding import PartitionSpec as P

BLOCK = 512
KMAX = 2
NEG = -1e30
F32 = jnp.float32
BF16 = jnp.bfloat16
VMEM_LIMIT = 16 * 1024 * 1024
VMEM = pl.BlockSpec(memory_space=pltpu.VMEM)
NZ, NY, NC = 4, 2, 2
NT = (((1,), (1,)), ((), ()))
NN = (((1,), (0,)), ((), ()))


def call(kernel, name, prefetch, grid, in_specs, out_specs, out_shape, scratch=(), flops=0, moved=0):
    return pl.pallas_call(
        kernel,
        grid_spec=pltpu.PrefetchScalarGridSpec(
            num_scalar_prefetch=prefetch,
            grid=grid,
            in_specs=in_specs,
            out_specs=out_specs,
            scratch_shapes=list(scratch),
        ),
        out_shape=out_shape,
        compiler_params=pltpu.CompilerParams(vmem_limit_bytes=VMEM_LIMIT),
        cost_estimate=pl.CostEstimate(flops=flops, bytes_accessed=moved, transcendentals=0),
        name=name,
    )


def dot(a, b, dims):
    return lax.dot_general(a, b, dims, preferred_element_type=F32)


class Meta:
    def __init__(self, tok_count, nblk):
        self.tok_count, self.nblk = tok_count, nblk

    def block(self, m, t, slot):
        return m[t * KMAX + slot]

    def kept(self, m, t):
        return m[self.tok_count * KMAX + t]

    def tok(self, m):
        return m[self.tok_count * (KMAX + 1)]

    def voc(self, m):
        return m[self.tok_count * (KMAX + 1) + 1]

    def core(self, m):
        return lax.rem(self.voc(m), NC)

    def y(self, m):
        return lax.rem(lax.div(self.voc(m), NC), NY)

    def count(self, m):
        return self.kept(m, self.tok(m))

    def start(self, m, slot):
        return (self.voc(m) * self.nblk + self.block(m, self.tok(m), slot)) * BLOCK

    def z(self, m):
        return lax.div(self.voc(m), NC * NY)

    def held(self, m, k, e):
        return lax.rem(self.z(m) + NZ - k, NZ) * NY + jnp.bitwise_xor(self.y(m), e)

    def owed(self, m, k, e):
        return lax.rem(self.z(m) + k, NZ) * NY + e


def gather_kernel(m, first, second, out):
    out[0, :BLOCK, :] = first[0]
    out[0, BLOCK:, :] = second[0]


def gather_call(meta, lists, weight):
    _, rows, columns = weight.shape
    shape = (meta.tok_count, KMAX * rows, columns)
    return call(
        gather_kernel,
        "gather",
        1,
        (meta.tok_count,),
        [
            pl.BlockSpec((1, rows, columns), lambda t, m, s=slot: (meta.block(m, t, s), 0, 0))
            for slot in range(KMAX)
        ],
        pl.BlockSpec((1, KMAX * rows, columns), lambda t, m: (t, 0, 0)),
        jax.ShapeDtypeStruct(shape, BF16),
        moved=4 * meta.tok_count * KMAX * rows * columns,
    )(lists, weight, weight)


def pair_kernel(hidden, near, tiles, frequent, out):
    del tiles, frequent
    out[0] = hidden[...]
    out[1] = near[...]


def pair_call(hidden, near, *behind):
    return call(
        pair_kernel,
        "pair",
        0,
        (),
        [VMEM, VMEM] + [pl.BlockSpec(memory_space=pl.ANY)] * len(behind),
        VMEM,
        jax.ShapeDtypeStruct((NY, *hidden.shape), hidden.dtype),
        moved=8 * hidden.size,
    )(hidden, near, *behind)


def hold(arrays, behind):
    n = len(arrays)
    anywhere = pl.BlockSpec(memory_space=pl.ANY)
    return pl.pallas_call(
        lambda *refs: None,
        in_specs=[anywhere] * (n + 1),
        out_specs=[anywhere] * n,
        out_shape=[jax.ShapeDtypeStruct(a.shape, a.dtype) for a in arrays],
        input_output_aliases={i: i for i in range(n)},
        compiler_params=pltpu.CompilerParams(vmem_limit_bytes=VMEM_LIMIT),
        name="hold",
    )(*arrays, behind)


def half_of(core, half):
    return pl.ds(pl.multiple_of(core * half, half), half)


def line_up(pieces, features):
    half = pieces[0].shape[-1]
    for k, piece in enumerate(pieces):
        for e in range(NY):
            features[:, (k * NY + e) * half : (k * NY + e + 1) * half] = piece[e]


def features_kernel(p0, p1, p2, p3, features):
    line_up((p0, p1, p2, p3), features)


def features_call(pieces):
    _, tokens, half = pieces[0].shape
    shape = (tokens, NZ * NY * half)
    return call(
        features_kernel,
        "features",
        0,
        (),
        [VMEM] * NZ,
        VMEM,
        jax.ShapeDtypeStruct(shape, BF16),
        moved=4 * shape[0] * shape[1],
    )(*pieces)


def products(meta, m, w, core, features, rows, slots):
    half = features.shape[-1] // (NZ * NY)
    places = [(k, e) for k in range(NZ) for e in range(NY)]
    for slot in range(slots):
        some = pl.ds(slot * BLOCK, BLOCK)
        for i, (k, e) in enumerate(places):
            rows[slot, :, i * half : (i + 1) * half] = w[meta.held(m, k, e), some, half_of(core, half)]
    return [dot(rows[slot], features[...], NT) for slot in range(slots)]


def near_kernel(meta, m, features, w, logits, rows):
    for n in range(1, KMAX + 1):

        @pl.when(meta.count(m) == n)
        def _(n=n):
            found = products(meta, m, w, meta.core(m), features, rows, n)
            for slot, values in enumerate(found):
                logits[pl.ds(slot * BLOCK, BLOCK), :] = values


def far_kernel(meta, m, p0, p1, p2, p3, w, near, logits, stats, features, rows):
    @pl.when(meta.count(m) == 0)
    def _():
        stats[0:1, :] = jnp.full(stats[0:1, :].shape, NEG, F32)
        stats[1:2, :] = jnp.zeros(stats[1:2, :].shape, F32)

    for n in range(1, KMAX + 1):

        @pl.when(meta.count(m) == n)
        def _(n=n):
            line_up((p0, p1, p2, p3), features)
            found = products(meta, m, w, 1 - meta.core(m), features, rows, n)
            tops, sums = [], []
            for slot, values in enumerate(found):
                some = pl.ds(slot * BLOCK, BLOCK)
                values = near[some, :] + values
                logits[some, :] = values
                tops.append(jnp.max(values, axis=0, keepdims=True))
                sums.append(jnp.sum(jnp.exp(values - tops[-1]), axis=0, keepdims=True))
            top = functools.reduce(jnp.maximum, tops)
            stats[0:1, :] = top
            stats[1:2, :] = sum(s * jnp.exp(t - top) for s, t in zip(sums, tops))


def logits_call(meta, m, pieces, w, near=None):
    chunks, width, columns = w.shape
    _, tokens, half = pieces[0].shape
    shape = jax.ShapeDtypeStruct((width, tokens), F32)
    far = near is not None
    return call(
        functools.partial(far_kernel if far else near_kernel, meta),
        "logits_far" if far else "logits_near",
        1,
        (),
        [VMEM] * (NZ + 2 if far else 2),
        [VMEM, VMEM] if far else VMEM,
        [shape, jax.ShapeDtypeStruct((2, tokens), F32)] if far else shape,
        [
            *[pltpu.VMEM((tokens, chunks * half), BF16)] * far,
            pltpu.VMEM((KMAX, BLOCK, chunks * half), BF16),
        ],
        flops=width * tokens * chunks * columns,
        moved=width * chunks * columns + 4 * width * tokens,
    )(m, *(pieces if far else [features_call(pieces)]), w, *[near] * far)


def other_kernel(meta, m, logits, s0, s1, s2, s3, cot, targets, w, grad_t, grad, other):
    count = meta.count(m)
    chunks, _, half = other.shape
    parts = [s0[...], s1[...], s2[...], s3[...]]
    top = functools.reduce(jnp.maximum, [s[0:1, :] for s in parts])
    lse = top + jnp.log(sum(s[1:2, :] * jnp.exp(s[0:1, :] - top) for s in parts))
    for slot in range(KMAX):
        rows = pl.ds(slot * BLOCK, BLOCK)

        @pl.when(slot < count)
        def _(slot=slot, rows=rows):
            prob = jnp.exp(logits[rows, :] - lse)
            place = lax.broadcasted_iota(jnp.int32, prob.shape, 0)
            hit = place == targets[...] - meta.start(m, slot)
            value = (cot[...] * (prob - jnp.where(hit, 1.0, 0.0))).astype(BF16)
            grad_t[rows, :] = value
            grad[:, rows] = value.T

    @pl.when(count == 0)
    def _():
        other[...] = jnp.zeros(other.shape, BF16)

    for n in range(1, KMAX + 1):

        @pl.when(count == n)
        def _(width=n * BLOCK):
            for c in range(chunks):
                rows = w[c, :width, half_of(1 - meta.core(m), half)]
                other[c] = dot(grad[:, :width], rows, NN).astype(BF16)


def other_call(meta, m, logits, stats, cot, targets, w):
    chunks, width, columns = w.shape
    tokens = logits.shape[1]
    return call(
        functools.partial(other_kernel, meta),
        "hidden_other",
        1,
        (),
        [VMEM] * 8,
        [VMEM] * 3,
        [
            jax.ShapeDtypeStruct((width, tokens), BF16),
            jax.ShapeDtypeStruct((tokens, width), BF16),
            jax.ShapeDtypeStruct((chunks, tokens, columns // NC), BF16),
        ],
        flops=width * tokens * chunks * columns,
        moved=w.size + 4 * logits.size,
    )(m, logits, *stats, cot, targets, w)


def rows_kernel(meta, m, grad_t, *refs):
    out = refs[-1]
    pieces, others = refs[:NZ], refs[NZ : 2 * NZ]
    half = pieces[0].shape[-1]
    core = meta.core(m)
    for n in range(1, KMAX + 1):

        @pl.when(meta.count(m) == n)
        def _(width=n * BLOCK):
            for k in range(NZ):
                for e in range(NY):
                    c = meta.held(m, k, e)
                    for side, piece in ((core, pieces[k]), (1 - core, others[k])):
                        value = dot(grad_t[:width, :], piece[e], NN)
                        out[c, :width, half_of(side, half)] = value.astype(BF16)


def rows_call(meta, m, grad_t, pieces, others):
    width, tokens = grad_t.shape
    half = pieces[0].shape[-1]
    chunks = NZ * NY
    return call(
        functools.partial(rows_kernel, meta),
        "head_rows",
        1,
        (),
        [VMEM] * (1 + 2 * NZ),
        VMEM,
        jax.ShapeDtypeStruct((chunks, width, NC * half), BF16),
        flops=2 * width * tokens * chunks * NC * half,
        moved=2 * chunks * width * NC * half,
    )(m, grad_t, *pieces, *others)


def mine_kernel(meta, m, grad, w, got, rows, *outs):
    del rows
    count = meta.count(m)
    half = got.shape[-1]
    for n in range(KMAX + 1):

        @pl.when(count == n)
        def _(width=n * BLOCK):
            for k, out in enumerate(outs):
                for e in range(NY):
                    c = meta.owed(m, k, e)
                    value = got[c].astype(F32)
                    if width:
                        own = w[c, :width, half_of(meta.core(m), half)]
                        value = value + dot(grad[:, :width], own, NN)
                    out[e] = value.astype(out.dtype)


def mine_call(meta, m, grad, w, got, rows):
    chunks, width, columns = w.shape
    tokens = grad.shape[0]
    shape = (NY, tokens, columns // NC)
    return call(
        functools.partial(mine_kernel, meta),
        "hidden_mine",
        1,
        (),
        [VMEM] * 3 + [pl.BlockSpec(memory_space=pl.ANY)],
        [VMEM] * NZ,
        [jax.ShapeDtypeStruct(shape, BF16 if k else F32) for k in range(NZ)],
        flops=width * tokens * chunks * columns,
        moved=w.size,
    )(m, grad, w, got, rows)


def combine_kernel(meta, m, pieces, out, total):
    block = pl.program_id(0)
    entries = [(t, slot) for t in range(meta.tok_count) for slot in range(KMAX)]
    here = [(meta.block(m, t, slot) == block) & (slot < meta.kept(m, t)) for t, slot in entries]
    number = sum(h.astype(jnp.int32) for h in here)
    first = functools.reduce(
        jnp.minimum, [jnp.where(h, i, len(entries) - 1) for i, h in enumerate(here)]
    )
    last = functools.reduce(jnp.maximum, [jnp.where(h, i, 0) for i, h in enumerate(here)])

    def piece(i):
        rows = pl.ds(pl.multiple_of(lax.rem(i, KMAX) * BLOCK, BLOCK), BLOCK)
        return pieces[lax.div(i, KMAX), rows, :]

    @pl.when(number == 0)
    def _():
        out[0] = jnp.zeros(total.shape, BF16)

    @pl.when(number == 1)
    def _():
        out[0] = piece(first)

    @pl.when(number == 2)
    def _():
        out[0] = (piece(first).astype(F32) + piece(last).astype(F32)).astype(BF16)

    @pl.when(number > 2)
    def _():
        total[...] = piece(first).astype(F32) + piece(last).astype(F32)
        for i, ((t, slot), found) in enumerate(zip(entries, here)):

            @pl.when(found & (i != first) & (i != last))
            def _(t=t, slot=slot):
                total[...] += pieces[t, slot * BLOCK : (slot + 1) * BLOCK, :].astype(F32)

        out[0] = total[...].astype(BF16)


def combine_call(meta, m, pieces):
    columns = pieces.shape[2]
    return call(
        functools.partial(combine_kernel, meta),
        "combine",
        1,
        (meta.nblk,),
        [VMEM],
        pl.BlockSpec((1, BLOCK, columns), lambda b, m: (b, 0, 0)),
        jax.ShapeDtypeStruct((meta.nblk, BLOCK, columns), BF16),
        [pltpu.VMEM((BLOCK, columns), F32)],
        moved=2 * pieces.size + 2 * meta.nblk * BLOCK * columns,
    )(m, pieces)


def pick_kernel(meta, m, *refs):
    *parts, _, keep, away = refs
    y = meta.y(m)
    keep[...] = functools.reduce(jnp.add, [p[y].astype(F32) for p in parts])
    away[...] = functools.reduce(jnp.add, [p[1 - y].astype(F32) for p in parts]).astype(BF16)


def pick_call(meta, m, parts, returned):
    _, tokens, half = parts[0].shape
    return call(
        functools.partial(pick_kernel, meta),
        "pick",
        1,
        (),
        [VMEM] * len(parts) + [pl.BlockSpec(memory_space=pl.ANY)],
        [VMEM, VMEM],
        [
            jax.ShapeDtypeStruct((tokens, half), F32),
            jax.ShapeDtypeStruct((tokens, half), BF16),
        ],
        moved=12 * NY * tokens * half,
    )(m, *parts, returned)


def merge(parts):
    top = functools.reduce(jnp.maximum, [s[0] for s in parts])
    return jnp.stack([top, sum(s[1] * jnp.exp(s[0] - top) for s in parts)])


def exchange(parts, frequent):
    def swap(x):
        return lax.all_to_all(x, "tok", split_axis=0, concat_axis=0, tiled=True)

    def small(x):
        rest = jnp.zeros((x.shape[0], x.shape[1] - BLOCK, x.shape[2]), x.dtype)
        return jnp.concatenate([swap(x[:, :BLOCK]), rest], axis=1)

    return lax.cond(frequent[0, 0] > 1, swap, small, parts)


def local(hidden, weight, targets, cotangent, kept_blocks, kept_counts):
    tok_count = lax.axis_size("tok")
    voc_count = lax.axis_size("voc")
    tok_me = lax.axis_index("tok")
    voc_me = lax.axis_index("voc")
    stride = NC * NY

    def flip(x, bits):
        return lax.ppermute(x, "voc", [(i, i ^ bits) for i in range(voc_count)])

    def up(x, k):
        pairs = [(i, (i + k * stride) % voc_count) for i in range(voc_count)]
        return lax.ppermute(x, "voc", pairs) if k else x

    vrows, columns = weight.shape
    nblk = vrows // BLOCK
    lists = kept_blocks[:, 0, :].reshape(-1)
    counts = kept_counts[:, 0]
    frequent = jnp.max(counts)[None, None]
    meta = Meta(tok_count, nblk)
    m = jnp.concatenate([lists, counts, jnp.stack([tok_me, voc_me])]).astype(jnp.int32)

    tiles = gather_call(meta, m, weight.reshape(nblk, BLOCK, columns))
    pair = pair_call(hidden, flip(hidden, NC), tiles, frequent)
    pieces = [up(pair, k) for k in range(NZ)]
    w = exchange(tiles, frequent)
    pieces = [pair, *hold(pieces[1:], w)]
    others = [flip(piece, 1) for piece in pieces]

    near = logits_call(meta, m, pieces, w)
    logits, stats = logits_call(meta, m, others, w, near)
    stats = merge([up(stats, k) for k in range(NZ)])
    stats = [stats] + [flip(stats, bits) for bits in (1, NC, NC + 1)]
    grad_t, grad, other = other_call(
        meta, m, logits, stats, cotangent[None, :], targets[None, :], w
    )
    got = flip(other, 1)
    rows = rows_call(meta, m, grad_t, pieces, others)
    owed = mine_call(meta, m, grad, w, got, rows)
    parts = [up(part, k) for k, part in enumerate(owed)]
    returned = exchange(rows, frequent)
    keep, away = pick_call(meta, m, parts, returned)
    d_weight = combine_call(meta, m, returned)
    d_hidden = (keep + flip(away, NC).astype(F32)).astype(BF16)
    return (d_hidden, d_weight.reshape(vrows, columns))


def solution(mesh):
    placed = (
        P("tok", "voc"),
        P("voc", "tok"),
        P("tok"),
        P("tok"),
        P(None, "voc", None),
        P(None, "voc"),
    )
    return jax.shard_map(
        local,
        mesh=mesh,
        in_specs=placed,
        out_specs=(P("tok", "voc"), P("voc", "tok")),
        check_vma=False,
    )
```
